256 devices in a mesh: dp: 4 (over x), expert: 64 (over z, y, core).
Axes of the slice: x: 4, y: 4, z: 8, core: 2. Of those that a mesh axis runs over, the one named last changes fastest.
Arguments:
- query_nope: bfloat16 [64, 128, 2048], P('expert', None, 'dp'), may hold values from -6 to 6
- query_rope: bfloat16 [64, 128, 1024], P('expert', None, 'dp'), may hold values from -8 to 8
- latent_new: bfloat16 [64, 128, 512], P('expert'), may hold values from -6 to 6
- key_rope: bfloat16 [64, 128, 64], P('expert'), may hold values from -8 to 8
- latent_pages: bfloat16 [64, 16, 64, 512], P('expert', 'dp'), may hold values from -6 to 6
- rope_pages: bfloat16 [64, 16, 4096], P('expert', 'dp'), may hold values from -6 to 6
- page_table: int32 [64, 16], P('expert'), may hold values from 0 to 15, each once within a row
- prefix_lengths: int32 [64], P('expert'), may hold values from 0 to 1024, as said below
- residual: bfloat16 [64, 128, 2048], P('expert'), may hold values from -60 to 60
- key_up: bfloat16 [16, 128, 512], P('dp'), may hold values from -0.5 to 0.5
- value_up: bfloat16 [16, 512, 128], P('dp'), may hold values from -0.25 to 0.25
- out_weight: bfloat16 [2048, 2048], P('dp'), may hold values from -0.125 to 0.125
- norm_gain: float32 [2048], replicated, may hold values from 0.1 to 1.9
- expert_in: bfloat16 [64, 1408, 2, 2048], P('expert', 'dp'), may hold values from -0.125 to 0.125
- expert_down: bfloat16 [64, 1408, 2048], P('expert', 'dp'), may hold values from -0.15625 to 0.15625
- expert_ids: int32 [64, 128, 6], P('expert'), may hold values from 0 to 63, all different within a row; in each aligned block of 32 rows (0 to 31, 32 to 63, ..., all dimensions but the last counted through in order) at most 6 rows name the same one
- expert_weights: float32 [64, 128, 6], P('expert'), may hold values from 0.05 to 0.4
Outputs:
- layer_out: bfloat16 [64, 128, 2048], P('expert', 'dp')
- expert_mix: bfloat16 [64, 128, 2048], P('expert', 'dp')
The draws below stay inside these ranges and needn't reach their ends.
Inputs may be any that keep to these rules, and one draw needn't show every extreme that they name: `prefix_lengths`: some request's prefix fills all of its 16 page slots. `page_table`: each row names every page slot of its request once; entry j holds positions j * 64 to (j + 1) * 64 - 1. `expert_ids`: each row names 6 distinct experts; in each aligned block of 32 rows of a request (blocks along the first two dimensions taken together) no expert is named more than 6 times, and that many is reached.
All inputs are finite; a program needn't handle non-finite values.
Results may differ from the reference program's by a relative error of at most 0.019.
Values may be sent and summed in bfloat16 or wider, within the bound.
No kernel may reach another device: no remote copies, remote signals or barrier semaphores. Data moves between devices by JAX's collectives and lax.ppermute only.
A program may use at most 128 MiB of HBM per device.

```python
import math
import jax
import jax.numpy as jnp
import numpy as np
from jax import lax

D = 2048
H = 16
HD = 128
RD = 64
LAT = 512
FFE = 1408
TOP = 6
PAGE = 64
T_COL = 128
EXPERTS = 64
REQS = 64
PAGES = 16
HSPLIT = 4
QROWS = 32
CAPQ = 6


def rope_pair(key):
    base_k = jnp.clip(jax.random.normal(jax.random.fold_in(key, 11), (REQS, T_COL, RD), jnp.float32), -6.0, 6.0)
    base_q = jnp.clip(jax.random.normal(jax.random.fold_in(key, 12), (REQS, T_COL, H * RD), jnp.float32), -6.0, 6.0)
    return (base_q, base_k)


def draw_query_rope(key, part):
    return rope_pair(key)[0].astype(jnp.bfloat16)


def draw_key_rope(key, part):
    return rope_pair(key)[1].astype(jnp.bfloat16)


def draw_residual(key, part):
    low = math.log(0.3)
    high = math.log(3.0)
    row_scale = jnp.exp(jax.random.uniform(jax.random.fold_in(key, 31), (REQS, T_COL, 1), jnp.float32, low, high))
    col_scale = jnp.exp(jax.random.uniform(jax.random.fold_in(key, 32), (1, 1, D), jnp.float32, low, high))
    base = jnp.clip(jax.random.normal(jax.random.fold_in(key, 33), (REQS, T_COL, D), jnp.float32), -5.0, 5.0)
    return (base * row_scale * col_scale).astype(jnp.bfloat16)


def draw_prefix_lengths(key, part):
    lengths = jax.random.randint(jax.random.fold_in(key, 21), (REQS,), 0, PAGES * PAGE + 1)
    full = jax.random.randint(jax.random.fold_in(key, 22), (), 0, REQS)
    return jnp.where(jnp.arange(REQS) == full, PAGES * PAGE, lengths).astype(jnp.int32)


def block_levels(key, extent, split, low, high):
    loudness = 1.0
    for dim, shards_of in split:
        draws = jax.random.uniform(jax.random.fold_in(jax.random.fold_in(key, 6), dim), (shards_of,), jnp.float32, low / len(split), high / len(split))
        loudness = loudness * jnp.repeat(jnp.exp(draws), extent[dim] // shards_of).reshape((-1,) + (1,) * (len(extent) - 1 - dim))
    return loudness


def deal_out(stream_key, own, number, rows, count, top, most, slope):
    sequence = jax.random.permutation(stream_key, count)
    crowded, usual = load_shares(count, rows * top, most, slope, True), load_shares(count, rows * top, most, slope, False)
    places = jnp.arange(count)

    def named(tallies, rotation):
        used = int((tallies > 0).sum())
        fixed = max(1, used // 4)
        moved = fixed + (places - fixed + rotation * (used - fixed)) % max(1, count - fixed)
        return jnp.zeros((count,), jnp.int32).at[sequence[jnp.where(places < fixed, places, moved)]].set(jnp.asarray(tallies, jnp.int32))

    tallies = jnp.where(number % 4 == 0, named(crowded, number // 4), named(usual, number - number // 4 - 1))
    mixed = jax.random.permutation(jax.random.fold_in(own, 3), count)
    giver, taker = mixed[0:count // 2 * 2:2], mixed[1:count // 2 * 2:2]
    room = jnp.minimum(tallies[giver] - 1, most - tallies[taker]) // 2
    room = jnp.where((giver == sequence[0]) | (taker == sequence[0]) | (tallies[taker] == 0), 0, jnp.maximum(room, 0))
    moved = jax.random.randint(jax.random.fold_in(own, 4), (count // 2,), 0, 1 << 20) % (room + 1)
    tallies = tallies.at[giver].add(-moved).at[taker].add(moved)
    members = jnp.searchsorted(jnp.cumsum(tallies), jnp.arange(rows * top), side="right").astype(jnp.int32)
    grid = members.reshape(top, rows).T
    grid = grid[jax.random.permutation(jax.random.fold_in(own, 1), rows)]
    rotation = jax.random.randint(jax.random.fold_in(own, 2), (rows, 1), 0, top)
    return jnp.take_along_axis(grid, (jnp.arange(top)[None, :] + rotation) % top, axis=1)


def load_shares(count, total, bound, slope, full):
    loads = [(1 << 20) // math.isqrt(grade ** slope) + 1 for grade in range(1, count + 1)]
    largest = bound if full else min(bound, max(-(-total // count), total * loads[0] // sum(loads)))
    least = 1 if total - largest >= count - 1 else 0
    counts, surplus = [largest] + [least] * (count - 1), total - largest - least * (count - 1)
    while surplus > 0:
        free = [i for i in range(1, count) if counts[i] < largest] or [i for i in range(1, count) if counts[i] < bound]
        whole, budget = sum([loads[i] for i in free]), surplus
        for i in free:
            addition = min(bound - counts[i], max(1, budget * loads[i] // whole), surplus)
            counts[i] = counts[i] + addition
            surplus = surplus - addition
    return np.array(counts)


def scatter_about(key, dims, spread, bound, pieces=(), held_as=jnp.bfloat16):
    array = jax.random.normal(key, dims, jnp.float32) * spread
    if len(pieces) > 0:
        array = block_levels(key, dims, pieces, -0.22, 0.18) * array
    return jnp.clip(array, min=-bound, max=bound).astype(held_as)


def setup_inputs(seed: int = 0) -> dict:
    streams_of = jax.random.split(jax.random.key(seed), 18)
    query_nope = scatter_about(streams_of[0], (REQS, T_COL, H * HD), 1.0, 6.0, ((0, 64), (2, 4)))
    query_rope = draw_query_rope(jax.random.fold_in(streams_of[17], 71), 0)
    latent_new = scatter_about(streams_of[2], (REQS, T_COL, LAT), 1.0, 6.0, ((0, 64),))
    key_rope = draw_key_rope(jax.random.fold_in(streams_of[17], 71), 0)
    latent_pages = scatter_about(streams_of[4], (REQS, PAGES, PAGE, LAT), 1.0, 6.0, ((0, 64), (1, 4)))
    rope_pages = scatter_about(streams_of[5], (REQS, PAGES, PAGE * RD), 1.0, 6.0, ((0, 64), (1, 4)))
    page_table = jax.vmap(lambda own: jax.random.permutation(own, PAGES))(jax.random.split(streams_of[6], REQS)).reshape((REQS, PAGES)).astype(jnp.int32)
    prefix_lengths = draw_prefix_lengths(jax.random.fold_in(streams_of[17], 71), 0)
    residual = draw_residual(jax.random.fold_in(streams_of[17], 71), 0)
    key_up = scatter_about(streams_of[9], (H, HD, LAT), HD ** -0.5, 0.5, ((0, 4),))
    value_up = scatter_about(streams_of[10], (H, LAT, HD), LAT ** -0.5, 0.25, ((0, 4),))
    out_weight = scatter_about(streams_of[11], (H * HD, D), (H * HD) ** -0.5, 0.125, ((0, 4),))
    norm_gain = jnp.clip(1.0 + 0.18 * jax.random.normal(streams_of[12], (D,), jnp.float32), 0.1, 1.9)
    expert_in = scatter_about(streams_of[13], (EXPERTS, FFE, 2, D), D ** -0.5, 0.125, ((0, 64), (1, 4)))
    expert_down = scatter_about(streams_of[14], (EXPERTS, FFE, D), FFE ** -0.5, 0.15625, ((0, 64), (1, 4)))
    expert_ids_keys = jax.random.split(jax.random.fold_in(streams_of[15], 1), REQS * T_COL // QROWS)
    expert_ids_turns = jax.random.permutation(jax.random.fold_in(streams_of[15], 3), REQS * T_COL // QROWS)
    expert_ids = jax.vmap(lambda own, number: deal_out(jax.random.fold_in(streams_of[15], 2), own, number, QROWS, EXPERTS, TOP, CAPQ, 2))(expert_ids_keys, expert_ids_turns).reshape((REQS, T_COL, TOP))
    expert_weights = jnp.clip(0.05 + 0.35 * jax.random.uniform(streams_of[16], (REQS, T_COL, TOP), jnp.float32) ** block_levels(streams_of[16], (REQS, T_COL, TOP), ((0, 64),), -0.2, 0.2), 0.05, 0.4)
    return {"query_nope": query_nope, "query_rope": query_rope, "latent_new": latent_new, "key_rope": key_rope, "latent_pages": latent_pages, "rope_pages": rope_pages, "page_table": page_table, "prefix_lengths": prefix_lengths, "residual": residual, "key_up": key_up, "value_up": value_up, "out_weight": out_weight, "norm_gain": norm_gain, "expert_in": expert_in, "expert_down": expert_down, "expert_ids": expert_ids, "expert_weights": expert_weights}


EPS = 1e-06
NEG = -1e+30

def rounded(value):
    return lax.optimization_barrier(value.astype(jnp.bfloat16)).astype(jnp.float32)

def reference(query_nope, query_rope, latent_new, key_rope, latent_pages, rope_pages, page_table, prefix_lengths, residual, key_up, value_up, out_weight, norm_gain, expert_in, expert_down, expert_ids, expert_weights):
    scale = 1.0 / (HD + RD) ** 0.5
    key_up_f = key_up.astype(jnp.float32)
    value_up_f = value_up.astype(jnp.float32)

    def attend(items):
        nope_rows, rope_rows, latent_rows, krope_rows, page_lat, page_rope, table, length, resid_rows = items
        heads_nope = nope_rows.reshape(T_COL, H, HD).astype(jnp.float32)
        query_lat = rounded(jnp.einsum('thd,hdc->thc', heads_nope, key_up_f))
        ordered_lat = page_lat[table].reshape(PAGES * PAGE, LAT)
        ordered_rope = page_rope[table].reshape(PAGES * PAGE, RD)
        keys_lat = jnp.concatenate([ordered_lat, latent_rows], axis=0).astype(jnp.float32)
        keys_rope = jnp.concatenate([ordered_rope, krope_rows], axis=0).astype(jnp.float32)
        heads_rope = rope_rows.reshape(T_COL, H, RD).astype(jnp.float32)
        scores = (jnp.einsum('thc,kc->thk', query_lat, keys_lat) + jnp.einsum('thr,kr->thk', heads_rope, keys_rope)) * scale
        prefix_ok = jnp.arange(PAGES * PAGE) < length
        causal = jnp.arange(T_COL)[None, :] <= jnp.arange(T_COL)[:, None]
        allowed = jnp.concatenate([jnp.broadcast_to(prefix_ok[None, :], (T_COL, PAGES * PAGE)), causal], axis=1)[:, None, :]
        masked = jnp.where(allowed, scores, NEG)
        peak = lax.optimization_barrier(jnp.max(masked, axis=-1, keepdims=True))
        expo = jnp.where(allowed, jnp.exp(masked - peak), 0.0)
        total = lax.optimization_barrier(jnp.sum(expo, axis=-1, keepdims=True))
        probs = rounded(expo)
        attn_latent = rounded(jnp.einsum('thk,kc->thc', probs, keys_lat) / total)
        heads_out = jnp.einsum('thc,hcd->thd', attn_latent, value_up_f).astype(jnp.bfloat16)
        attn = jnp.dot(heads_out.reshape(T_COL, H * HD), out_weight, preferred_element_type=jnp.float32)
        return resid_rows.astype(jnp.float32) + attn
    hidden = lax.map(attend, (query_nope, query_rope, latent_new, key_rope, latent_pages, rope_pages, page_table, prefix_lengths, residual))
    rows = REQS * T_COL
    flat_hidden = hidden.reshape(rows, D)
    power = lax.optimization_barrier(jnp.mean(flat_hidden * flat_hidden, axis=-1, keepdims=True))
    normed = (flat_hidden * lax.rsqrt(power + EPS) * norm_gain).astype(jnp.bfloat16)
    flat_ids = expert_ids.reshape(rows * TOP)
    flat_gates = expert_weights.reshape(rows * TOP)
    onehot = (flat_ids[:, None] == jnp.arange(EXPERTS)[None, :]).astype(jnp.int32)
    before = jnp.cumsum(onehot, axis=0) - onehot
    rank = lax.optimization_barrier(jnp.sum(before * onehot, axis=1)).astype(jnp.int32)
    capacity = REQS * HSPLIT * CAPQ
    group_width = FFE // HSPLIT
    source_row = (jnp.arange(rows * TOP) // TOP).astype(jnp.int32)

    def add_expert(mixture, expert):
        chosen = flat_ids == expert
        slot = jnp.where(chosen, rank, capacity).astype(jnp.int32)
        row_of = jnp.zeros((capacity,), jnp.int32).at[slot].set(source_row, mode='drop')
        gate_of = jnp.zeros((capacity,), jnp.float32).at[slot].set(flat_gates, mode='drop')
        picked = normed[row_of]
        rows_in = expert_in[expert]
        rows_down = expert_down[expert]
        result = jnp.zeros((capacity, D), jnp.float32)
        for group in range(HSPLIT):
            lower = group * group_width
            upper = lower + group_width
            gate_act = jnp.dot(picked, rows_in[lower:upper, 0, :].T, preferred_element_type=jnp.float32)
            up_act = jnp.dot(picked, rows_in[lower:upper, 1, :].T, preferred_element_type=jnp.float32)
            units = (jax.nn.silu(gate_act) * up_act).astype(jnp.bfloat16)
            part = jnp.dot(units, rows_down[lower:upper], preferred_element_type=jnp.float32).astype(jnp.bfloat16)
            result = result + part.astype(jnp.float32)
        mixture = mixture.at[row_of].add(result * gate_of[:, None])
        return (mixture, None)
    mixture, unused = lax.scan(add_expert, jnp.zeros((rows, D), jnp.float32), jnp.arange(EXPERTS))
    layer_out = (flat_hidden + mixture).astype(jnp.bfloat16).reshape(REQS, T_COL, D)
    expert_mix = mixture.astype(jnp.bfloat16).reshape(REQS, T_COL, D)
    return (layer_out, expert_mix)
```

```python
import functools

import jax
import jax.numpy as jnp
from jax import lax
from jax.experimental import pallas as pl
from jax.experimental.pallas import tpu as pltpu
from jax.sharding import PartitionSpec as P

HD = 128
RD = 64
LAT = 512
TOP = 6
PAGE = 64
EPS = 1e-06
NEG = -1e30

QUARTERS = 4
PAIR = 2
TILE = QUARTERS * PAIR
BLOCK = 256
BF = jnp.bfloat16
F32 = jnp.float32


def mm(a, b):
    return jnp.dot(a, b, preferred_element_type=F32)


def mm_nt(a, b):
    return lax.dot_general(a, b, (((1,), (1,)), ((), ())), preferred_element_type=F32)


def mm_tn(a, b):
    return lax.dot_general(a, b, (((0,), (0,)), ((), ())), preferred_element_type=F32)


def vmem(n):
    return [pl.BlockSpec(memory_space=pltpu.VMEM) for _ in range(n)]


def params(mib):
    return pltpu.CompilerParams(vmem_limit_bytes=mib * 2**20)


def attend_kernel(qn, qr, ku, k0, k1, k2, k3, kn, bias, vu, ow, out, q_scr, ho_scr):
    tokens = qn.shape[0]
    heads = ku.shape[0]
    width = q_scr.shape[1]
    for h in range(heads):
        rows = pl.ds(h * tokens, tokens)
        q_scr[rows, 0:LAT] = mm(qn[:, h * HD : (h + 1) * HD], ku[h]).astype(BF)
        rope = qr[:, h * RD : (h + 1) * RD]
        q_scr[rows, LAT:width] = jnp.concatenate(
            [rope, jnp.zeros((tokens, width - LAT - RD), BF)], axis=1
        )
    scale = 1.0 / (HD + RD) ** 0.5
    keys = (k0, k1, k2, k3)
    span = k0.shape[0]
    step = 2
    for h0 in range(0, heads, step):
        n = step * tokens
        q = q_scr[pl.ds(h0 * tokens, n), :]
        row = lax.rem(lax.broadcasted_iota(jnp.int32, (n, tokens), 0), tokens)
        col = lax.broadcasted_iota(jnp.int32, (n, tokens), 1)
        s_new = jnp.where(col <= row, mm_nt(q, kn[...]) * scale, NEG)
        s_old = [
            mm_nt(q, k[...]) * scale + bias[:, i * span : (i + 1) * span]
            for i, k in enumerate(keys)
        ]
        peak = jnp.max(s_new, axis=1, keepdims=True)
        for s in s_old:
            peak = jnp.maximum(peak, jnp.max(s, axis=1, keepdims=True))
        e = jnp.exp(s_new - peak)
        total = jnp.sum(e, axis=1, keepdims=True)
        acc = mm(e.astype(BF), kn[:, 0:LAT])
        for s, k in zip(s_old, keys):
            e = jnp.exp(s - peak)
            total = total + jnp.sum(e, axis=1, keepdims=True)
            acc = acc + mm(e.astype(BF), k[:, 0:LAT])
        latent = (acc / total).astype(BF)
        for i in range(step):
            ho_scr[:, (h0 + i) * HD : (h0 + i + 1) * HD] = mm(
                latent[i * tokens : (i + 1) * tokens], vu[h0 + i]
            ).astype(BF)
    for c in range(0, out.shape[1], 512):
        out[:, c : c + 512] = mm(ho_scr[...], ow[:, c : c + 512]).astype(BF)


def route_kernel(ids, gates, pick, high, low):
    experts = pick.shape[1] // TILE
    lanes = ids.shape[1]
    block = lanes // QUARTERS
    expert = lax.broadcasted_iota(jnp.int32, (experts, lanes), 0)
    named = jnp.zeros((experts, lanes), F32)
    gate = jnp.zeros((experts, lanes), F32)
    for k in range(TOP):
        hit = (ids[k : k + 1, :] == expert).astype(F32)
        named = named + hit
        gate = gate + hit * gates[k : k + 1, :]
    a = lax.broadcasted_iota(jnp.int32, (lanes, lanes), 0)
    b = lax.broadcasted_iota(jnp.int32, (lanes, lanes), 1)
    earlier = ((a // block == b // block) & (a < b)).astype(BF)
    rank = mm(named.astype(BF), earlier)
    rank = jnp.where(named > 0, rank, -1.0).astype(BF)
    gate_high = gate.astype(BF)
    gate_low = (gate - gate_high.astype(F32)).astype(BF)
    total = experts * TILE
    r = lax.broadcasted_iota(jnp.int32, (total, experts), 0)
    c = lax.broadcasted_iota(jnp.int32, (total, experts), 1)
    spread = (r // TILE == c).astype(BF)
    rank_r = mm(spread, rank)
    high_r = mm(spread, gate_high)
    low_r = mm(spread, gate_low)
    row = lax.broadcasted_iota(jnp.int32, (total, lanes), 0)
    lane = lax.broadcasted_iota(jnp.int32, (total, lanes), 1)
    same = lax.rem(row, TILE) // PAIR == lane // block
    slot = lax.rem(row, PAIR)
    for i in range(pick.shape[0]):
        on = same & (rank_r == (slot + i * PAIR).astype(F32))
        pick[i] = jnp.where(on, 1.0, 0.0).astype(BF)
        high[i] = jnp.where(on, high_r, 0.0).astype(BF)
        low[i] = jnp.where(on, low_r, 0.0).astype(BF)


def pack_kernel(partial, residual, gain, pick, hidden_out, *outgoing):
    hidden = residual[...].astype(F32)
    attended = partial[0].astype(F32)
    for i in range(1, partial.shape[0]):
        attended = attended + partial[i].astype(F32)
    hidden = hidden + attended
    hidden_out[...] = hidden
    power = jnp.mean(hidden * hidden, axis=1, keepdims=True)
    normed = (hidden * lax.rsqrt(power + EPS) * gain[...]).astype(BF)
    w = normed.shape[1] // QUARTERS
    stacked = jnp.concatenate([normed[:, q * w : (q + 1) * w] for q in range(QUARTERS)], axis=0)
    for i, out in enumerate(outgoing):
        out[...] = mm(pick[i], stacked).astype(BF)


def reorder(transposed):
    i = lax.broadcasted_iota(jnp.int32, (BLOCK, BLOCK), 1 if transposed else 0)
    j = lax.broadcasted_iota(jnp.int32, (BLOCK, BLOCK), 0 if transposed else 1)
    group = BLOCK // QUARTERS
    rest = lax.rem(i, group)
    source = (rest // PAIR) * TILE + (i // group) * PAIR + lax.rem(rest, PAIR)
    return (j == source).astype(BF)


def hidden_units(x, w):
    n = w.shape[0] // 3
    gate = mm_nt(x, w[0:n, :])
    up = mm_nt(x, w[n : 2 * n, :])
    return (gate / (1.0 + jnp.exp(-gate)) * up).astype(BF)


def expert_kernel(x0, xl, xr, wa, wb, ra, rb, y0, yl, yr, rows, acc):
    n = wa.shape[0] // 3
    there = reorder(False)
    back = reorder(True)
    group = BLOCK // QUARTERS
    w = x0.shape[1]
    blocks = x0.shape[0] // BLOCK
    each = blocks * group
    for i, x in enumerate((x0, xl, xr)):
        for b in range(blocks):
            sorted_rows = mm(there, x[b * BLOCK : (b + 1) * BLOCK, :]).astype(BF)
            for q in range(QUARTERS):
                rows[pl.ds(i * each + b * group, group), q * w : (q + 1) * w] = sorted_rows[
                    q * group : (q + 1) * group
                ]
    ua = hidden_units(rows[...], wa)
    ub = hidden_units(rows[...], wb)
    acc[...] = mm(ua, wa[2 * n : 3 * n, :]) + mm(ub, wb[2 * n : 3 * n, :])
    for i, extra in ((1, ra), (2, rb)):
        part = pl.ds(i * each, each)
        u = hidden_units(rows[part, :], extra)
        acc[part, :] += mm(u, extra[2 * n : 3 * n, :])
    for i, y in enumerate((y0, yl, yr)):
        for b in range(blocks):
            part = acc[pl.ds(i * each + b * group, group), :].astype(BF)
            stacked = jnp.concatenate(
                [part[:, q * w : (q + 1) * w] for q in range(QUARTERS)], axis=0
            )
            y[b * BLOCK : (b + 1) * BLOCK, :] = mm(back, stacked).astype(BF)


def combine_kernel(hidden, high, low, *rest):
    returned, (layer_out, mix_out) = rest[:-2], rest[-2:]
    mixed = None
    for i, r in enumerate(returned):
        term = mm_tn(high[i], r[...]) + mm_tn(low[i], r[...])
        mixed = term if mixed is None else mixed + term
    block = mixed.shape[0] // QUARTERS
    w = mixed.shape[1]
    for q in range(QUARTERS):
        part = mixed[q * block : (q + 1) * block]
        cols = slice(q * w, (q + 1) * w)
        mix_out[:, cols] = part.astype(BF)
        layer_out[:, cols] = (hidden[:, cols] + part).astype(BF)


def per_device(
    query_nope,
    query_rope,
    latent_new,
    key_rope,
    latent_pages,
    rope_pages,
    page_table,
    prefix_lengths,
    residual,
    key_up,
    value_up,
    out_weight,
    norm_gain,
    expert_in,
    expert_down,
    expert_ids,
    expert_weights,
):
    groups = lax.axis_size("dp")
    experts = lax.axis_size("expert")
    me = lax.axis_index("dp")
    tokens, width = residual.shape[1:]
    block = tokens // groups
    pages_here = latent_pages.shape[1]
    span = pages_here * PAGE
    pages = pages_here * groups
    chunks = 3
    rows = experts * TILE
    quarter = width // QUARTERS
    shape = jax.ShapeDtypeStruct

    def shift(x, k):
        return lax.ppermute(x, "dp", [(i, (i + k) % groups) for i in range(groups)])

    pad = LAT // 4 - RD
    keys = jnp.concatenate(
        [
            latent_pages[0].reshape(span, LAT),
            rope_pages[0].reshape(span, RD),
            jnp.zeros((span, pad), BF),
        ],
        axis=1,
    )
    keys_new = jnp.concatenate([latent_new[0], key_rope[0], jnp.zeros((tokens, pad), BF)], axis=1)
    from_left, from_right, from_far = shift(keys, 1), shift(keys, -1), shift(keys, 2)

    holders = lax.rem(me + jnp.array([0, 3, 1, 2], jnp.int32), groups)
    slot = (holders[:, None] * pages_here + jnp.arange(pages_here)[None, :]).reshape(-1)
    place = jnp.sum(
        jnp.where(page_table[0][None, :] == slot[:, None], jnp.arange(pages)[None, :], 0), axis=1
    )
    position = place[:, None] * PAGE + jnp.arange(PAGE)[None, :]
    bias = jnp.where(position < prefix_lengths[0], 0.0, NEG).astype(F32).reshape(1, span * groups)

    start = me * block
    ids = lax.dynamic_slice_in_dim(expert_ids[0], start, block, 0)
    gates = lax.dynamic_slice_in_dim(expert_weights[0], start, block, 0)
    residual_mine = lax.dynamic_slice_in_dim(residual[0], start, block, 0)
    lanes = block * QUARTERS
    pick, high, low = pl.pallas_call(
        route_kernel,
        out_shape=[shape((chunks, rows, lanes), BF)] * 3,
        in_specs=vmem(2),
        out_specs=vmem(3),
        compiler_params=params(32),
        name="route",
    )(jnp.tile(ids.T, (1, QUARTERS)), jnp.tile(gates.T, (1, QUARTERS)))

    half = expert_in.shape[1] // 2

    def half_weights(i):
        part = slice(i * half, (i + 1) * half)
        return jnp.concatenate(
            [expert_in[0, part, 0, :], expert_in[0, part, 1, :], expert_down[0, part, :]], axis=0
        )

    wa, wb = half_weights(0), half_weights(1)
    ra, rb = shift(wa, -1), shift(wb, 1)

    partial = pl.pallas_call(
        attend_kernel,
        out_shape=shape((tokens, width), BF),
        in_specs=vmem(11),
        out_specs=vmem(1)[0],
        scratch_shapes=[
            pltpu.VMEM((key_up.shape[0] * tokens, keys.shape[1]), BF),
            pltpu.VMEM((tokens, key_up.shape[0] * HD), BF),
        ],
        compiler_params=params(48),
        name="attend",
    )(
        query_nope[0],
        query_rope[0],
        key_up,
        keys,
        from_left,
        from_right,
        from_far,
        keys_new,
        bias,
        value_up,
        out_weight,
    )
    partial = lax.all_to_all(
        partial.reshape(groups, block, width), "dp", split_axis=0, concat_axis=0, tiled=True
    )
    hidden, *outgoing = pl.pallas_call(
        pack_kernel,
        out_shape=[shape((block, width), F32)] + [shape((rows, quarter), BF)] * chunks,
        in_specs=vmem(4),
        out_specs=vmem(1 + chunks),
        compiler_params=params(32),
        name="pack",
    )(partial, residual_mine, norm_gain.reshape(1, width), pick)

    def swap(x):
        x = x.reshape(experts, TILE, quarter)
        x = lax.all_to_all(x, "expert", split_axis=0, concat_axis=0, tiled=True)
        return x.reshape(rows, quarter)

    each = rows // QUARTERS
    expert_call = pl.pallas_call(
        expert_kernel,
        out_shape=[shape((rows, quarter), BF)] * 3,
        in_specs=vmem(7),
        out_specs=vmem(3),
        scratch_shapes=[pltpu.VMEM((3 * each, width), BF), pltpu.VMEM((3 * each, width), F32)],
        compiler_params=params(48),
        name="experts",
    )
    arrived = [swap(x) for x in outgoing]
    returned = []
    for x in arrived:
        own, left, right = expert_call(x, shift(x, 1), shift(x, -1), wa, wb, ra, rb)
        total = own.astype(F32) + shift(left, -1).astype(F32) + shift(right, 1).astype(F32)
        returned.append(swap(total.astype(BF)))

    layer_out, mix = pl.pallas_call(
        combine_kernel,
        out_shape=[shape((block, width), BF)] * 2,
        in_specs=vmem(3 + chunks),
        out_specs=vmem(2),
        compiler_params=params(32),
        name="combine",
    )(hidden, high, low, *returned)
    return layer_out[None], mix[None]


def solution(mesh):
    return jax.shard_map(
        per_device,
        mesh=mesh,
        in_specs=(
            P("expert", None, "dp"),
            P("expert", None, "dp"),
            P("expert", None, None),
            P("expert", None, None),
            P("expert", "dp", None, None),
            P("expert", "dp", None),
            P("expert", None),
            P("expert"),
            P("expert", None, None),
            P("dp", None, None),
            P("dp", None, None),
            P("dp", None),
            P(),
            P("expert", "dp", None, None),
            P("expert", "dp", None),
            P("expert", None, None),
            P("expert", None, None),
        ),
        out_specs=(P("expert", "dp", None), P("expert", "dp", None)),
        check_vma=False,
    )
```

```python
import jax
import jax.numpy as jnp
from jax import lax
from jax.experimental import pallas as pl
from jax.experimental.pallas import tpu as pltpu
from jax.sharding import PartitionSpec as P

HD = 128
RD = 64
LAT = 512
TOP = 6
PAGE = 64
EPS = 1e-06
NEG = -1e30

PIECES = 8
SLOTS = 3
TILE = PIECES * SLOTS
SOURCES = 16
BLOCK = SOURCES * TILE
BF = jnp.bfloat16
F32 = jnp.float32


def mm(a, b):
    return jnp.dot(a, b, preferred_element_type=F32)


def mm_nt(a, b):
    return lax.dot_general(a, b, (((1,), (1,)), ((), ())), preferred_element_type=F32)


def mm_tn(a, b):
    return lax.dot_general(a, b, (((0,), (0,)), ((), ())), preferred_element_type=F32)


def vmem(n):
    return [pl.BlockSpec(memory_space=pltpu.VMEM) for _ in range(n)]


def params(mib):
    return pltpu.CompilerParams(vmem_limit_bytes=mib * 2**20)


def attend_kernel(qn, qr, ku, k0, k1, k2, k3, kn, bias, vu, ow, out, q_scr, ho_scr):
    tokens = qn.shape[0]
    heads = ku.shape[0]
    width = q_scr.shape[1]
    for h in range(heads):
        rows = pl.ds(h * tokens, tokens)
        q_scr[rows, 0:LAT] = mm(qn[:, h * HD : (h + 1) * HD], ku[h]).astype(BF)
        rope = qr[:, h * RD : (h + 1) * RD]
        q_scr[rows, LAT:width] = jnp.concatenate(
            [rope, jnp.zeros((tokens, width - LAT - RD), BF)], axis=1
        )
    scale = 1.0 / (HD + RD) ** 0.5
    keys = (k0, k1, k2, k3)
    span = k0.shape[0]
    step = 2
    for h0 in range(0, heads, step):
        n = step * tokens
        q = q_scr[pl.ds(h0 * tokens, n), :]
        row = lax.rem(lax.broadcasted_iota(jnp.int32, (n, tokens), 0), tokens)
        col = lax.broadcasted_iota(jnp.int32, (n, tokens), 1)
        s_new = jnp.where(col <= row, mm_nt(q, kn[...]) * scale, NEG)
        s_old = [
            mm_nt(q, k[...]) * scale + bias[:, i * span : (i + 1) * span]
            for i, k in enumerate(keys)
        ]
        peak = jnp.max(s_new, axis=1, keepdims=True)
        for s in s_old:
            peak = jnp.maximum(peak, jnp.max(s, axis=1, keepdims=True))
        e = jnp.exp(s_new - peak)
        total = jnp.sum(e, axis=1, keepdims=True)
        acc = mm(e.astype(BF), kn[:, 0:LAT])
        for s, k in zip(s_old, keys):
            e = jnp.exp(s - peak)
            total = total + jnp.sum(e, axis=1, keepdims=True)
            acc = acc + mm(e.astype(BF), k[:, 0:LAT])
        latent = (acc / total).astype(BF)
        for i in range(step):
            ho_scr[:, (h0 + i) * HD : (h0 + i + 1) * HD] = mm(
                latent[i * tokens : (i + 1) * tokens], vu[h0 + i]
            ).astype(BF)
    for c in range(0, out.shape[1], 512):
        out[:, c : c + 512] = mm(ho_scr[...], ow[:, c : c + 512]).astype(BF)


def count_named(ids, experts):
    block = ids.shape[1]
    expert = lax.broadcasted_iota(jnp.int32, (experts, block), 0)
    named = jnp.zeros((experts, block), F32)
    for k in range(TOP):
        named = named + (ids[k : k + 1, :] == expert).astype(F32)
    a = lax.broadcasted_iota(jnp.int32, (block, block), 0)
    b = lax.broadcasted_iota(jnp.int32, (block, block), 1)
    rank = mm(named.astype(BF), (a < b).astype(BF))
    return jnp.where(named > 0, rank, -1.0)


def reorder(transposed):
    i = lax.broadcasted_iota(jnp.int32, (BLOCK, BLOCK), 1 if transposed else 0)
    j = lax.broadcasted_iota(jnp.int32, (BLOCK, BLOCK), 0 if transposed else 1)
    piece, rest = i // (SLOTS * SOURCES), lax.rem(i, SLOTS * SOURCES)
    source = lax.rem(rest, SOURCES) * TILE + piece * SLOTS + rest // SOURCES
    return (j == source).astype(BF)


def unpack_rows(there, x, rows, base):
    w = x.shape[1]
    sources = x.shape[0] // TILE
    for b in range(sources // SOURCES):
        out = mm(there, x[b * BLOCK : (b + 1) * BLOCK, :]).astype(BF)
        for p in range(PIECES):
            for s in range(SLOTS):
                at = (p * SLOTS + s) * SOURCES
                rows[pl.ds(base + s * sources + b * SOURCES, SOURCES), p * w : (p + 1) * w] = out[
                    at : at + SOURCES
                ]


def pack_rows(back, rows, base, y):
    w = y.shape[1]
    sources = y.shape[0] // TILE
    for b in range(sources // SOURCES):
        stacked = jnp.concatenate(
            [
                rows[
                    pl.ds(base + s * sources + b * SOURCES, SOURCES), p * w : (p + 1) * w
                ].astype(BF)
                for p in range(PIECES)
                for s in range(SLOTS)
            ],
            axis=0,
        )
        y[b * BLOCK : (b + 1) * BLOCK, :] = mm(back, stacked).astype(BF)


def pack_kernel(partial, residual, gain, ids, hidden_out, *rest):
    outgoing, rows = rest[:-1], rest[-1]
    experts = outgoing[0].shape[0] // TILE
    hidden = residual[...].astype(F32)
    attended = partial[0].astype(F32)
    for i in range(1, partial.shape[0]):
        attended = attended + partial[i].astype(F32)
    hidden = hidden + attended
    hidden_out[...] = hidden
    power = jnp.mean(hidden * hidden, axis=1, keepdims=True)
    normed = (hidden * lax.rsqrt(power + EPS) * gain[...]).astype(BF)
    rank = count_named(ids, experts)
    back = reorder(True)
    for i, out in enumerate(outgoing):
        for s in range(SLOTS):
            pick = (rank == float(i * SLOTS + s)).astype(BF)
            rows[pl.ds(s * experts, experts), :] = mm(pick, normed).astype(BF)
        pack_rows(back, rows, 0, out)


def hidden_units(x, w):
    n = w.shape[0] // 3
    gate = mm_nt(x, w[0:n, :])
    up = mm_nt(x, w[n : 2 * n, :])
    return (gate / (1.0 + jnp.exp(-gate)) * up).astype(BF)


def down(units, w):
    n = w.shape[0] // 3
    return mm(units, w[2 * n : 3 * n, :])


def near_kernel(xl, xr, wa, wb, ra, rb, yl, yr, rows, acc):
    each = rows.shape[0] // 2
    there, back = reorder(False), reorder(True)
    for i, x in enumerate((xl, xr)):
        unpack_rows(there, x, rows, i * each)
    acc[...] = down(hidden_units(rows[...], wa), wa) + down(hidden_units(rows[...], wb), wb)
    for i, (extra, y) in enumerate(((ra, yl), (rb, yr))):
        part = pl.ds(i * each, each)
        acc[part, :] += down(hidden_units(rows[part, :], extra), extra)
        pack_rows(back, acc, i * each, y)


def own_kernel(x, wa, wb, y, rows, acc):
    there, back = reorder(False), reorder(True)
    unpack_rows(there, x, rows, 0)
    acc[...] = down(hidden_units(rows[...], wa), wa) + down(hidden_units(rows[...], wb), wb)
    pack_rows(back, acc, 0, y)


def combine_kernel(hidden, ids, gates, *rest):
    returned, (layer_out, mix_out, rows) = rest[:-3], rest[-3:]
    experts = returned[0].shape[0] // TILE
    rank = count_named(ids, experts)
    expert = lax.broadcasted_iota(jnp.int32, rank.shape, 0)
    gate = jnp.zeros(rank.shape, F32)
    for k in range(TOP):
        gate = gate + jnp.where(ids[k : k + 1, :] == expert, gates[k : k + 1, :], 0.0)
    there = reorder(False)
    mixed = None
    for i, r in enumerate(returned):
        unpack_rows(there, r, rows, 0)
        for s in range(SLOTS):
            here = jnp.where(rank == float(i * SLOTS + s), gate, 0.0)
            high = here.astype(BF)
            low = (here - high.astype(F32)).astype(BF)
            part = rows[pl.ds(s * experts, experts), :]
            term = mm_tn(high, part) + mm_tn(low, part)
            mixed = term if mixed is None else mixed + term
    mix_out[...] = mixed.astype(BF)
    layer_out[...] = (hidden[...] + mixed).astype(BF)


def per_device(
    query_nope,
    query_rope,
    latent_new,
    key_rope,
    latent_pages,
    rope_pages,
    page_table,
    prefix_lengths,
    residual,
    key_up,
    value_up,
    out_weight,
    norm_gain,
    expert_in,
    expert_down,
    expert_ids,
    expert_weights,
):
    groups = lax.axis_size("dp")
    experts = lax.axis_size("expert")
    me = lax.axis_index("dp")
    tokens, width = residual.shape[1:]
    block = tokens // groups
    pages_here = latent_pages.shape[1]
    span = pages_here * PAGE
    pages = pages_here * groups
    chunks = TOP // SLOTS
    rows = experts * TILE
    piece = width // PIECES
    shape = jax.ShapeDtypeStruct

    def shift(x, k):
        return lax.ppermute(x, "dp", [(i, (i + k) % groups) for i in range(groups)])

    pad = LAT // 4 - RD
    keys = jnp.concatenate(
        [
            latent_pages[0].reshape(span, LAT),
            rope_pages[0].reshape(span, RD),
            jnp.zeros((span, pad), BF),
        ],
        axis=1,
    )
    keys_new = jnp.concatenate([latent_new[0], key_rope[0], jnp.zeros((tokens, pad), BF)], axis=1)
    from_left, from_right, from_far = shift(keys, 1), shift(keys, -1), shift(keys, 2)

    holders = lax.rem(me + jnp.array([0, 3, 1, 2], jnp.int32), groups)
    slot = (holders[:, None] * pages_here + jnp.arange(pages_here)[None, :]).reshape(-1)
    place = jnp.sum(
        jnp.where(page_table[0][None, :] == slot[:, None], jnp.arange(pages)[None, :], 0), axis=1
    )
    position = place[:, None] * PAGE + jnp.arange(PAGE)[None, :]
    bias = jnp.where(position < prefix_lengths[0], 0.0, NEG).astype(F32).reshape(1, span * groups)

    start = me * block
    ids = lax.dynamic_slice_in_dim(expert_ids[0], start, block, 0)
    gates = lax.dynamic_slice_in_dim(expert_weights[0], start, block, 0)
    residual_mine = lax.dynamic_slice_in_dim(residual[0], start, block, 0)
    ids, gates = ids.T, gates.T

    half = expert_in.shape[1] // 2

    def half_weights(i):
        part = slice(i * half, (i + 1) * half)
        return jnp.concatenate(
            [expert_in[0, part, 0, :], expert_in[0, part, 1, :], expert_down[0, part, :]], axis=0
        )

    wa, wb = half_weights(0), half_weights(1)

    partial = pl.pallas_call(
        attend_kernel,
        out_shape=shape((tokens, width), BF),
        in_specs=vmem(11),
        out_specs=vmem(1)[0],
        scratch_shapes=[
            pltpu.VMEM((key_up.shape[0] * tokens, keys.shape[1]), BF),
            pltpu.VMEM((tokens, key_up.shape[0] * HD), BF),
        ],
        compiler_params=params(24),
        name="attend",
    )(
        query_nope[0],
        query_rope[0],
        key_up,
        keys,
        from_left,
        from_right,
        from_far,
        keys_new,
        bias,
        value_up,
        out_weight,
    )
    partial = lax.all_to_all(
        partial.reshape(groups, block, width), "dp", split_axis=0, concat_axis=0, tiled=True
    )
    send_a, send_b, partial = lax.optimization_barrier((wa, wb, partial))
    ra, rb = shift(send_a, -1), shift(send_b, 1)
    hidden, *outgoing = pl.pallas_call(
        pack_kernel,
        out_shape=[shape((block, width), F32)] + [shape((rows, piece), BF)] * chunks,
        in_specs=vmem(4),
        out_specs=vmem(1 + chunks),
        scratch_shapes=[pltpu.VMEM((SLOTS * experts, width), BF)],
        compiler_params=params(16),
        name="pack",
    )(partial, residual_mine, norm_gain.reshape(1, width), ids)

    def swap(x):
        x = x.reshape(experts, TILE, piece)
        x = lax.all_to_all(x, "expert", split_axis=0, concat_axis=0, tiled=True)
        return x.reshape(rows, piece)

    each = SLOTS * experts

    def experts_on(kernel, n_in, n_out, name):
        return pl.pallas_call(
            kernel,
            out_shape=[shape((rows, piece), BF)] * n_out,
            in_specs=vmem(n_in),
            out_specs=vmem(n_out),
            scratch_shapes=[
                pltpu.VMEM((n_out * each, width), BF),
                pltpu.VMEM((n_out * each, width), F32),
            ],
            compiler_params=params(32),
            name=name,
        )

    near = experts_on(near_kernel, 6, 2, "near_experts")
    own = experts_on(own_kernel, 3, 1, "own_experts")
    arrived = [swap(x) for x in outgoing]
    returned = []
    for x in arrived:
        left, right = near(shift(x, 1), shift(x, -1), wa, wb, ra, rb)
        (mine,) = own(x, wa, wb)
        total = mine.astype(F32) + shift(left, -1).astype(F32) + shift(right, 1).astype(F32)
        returned.append(swap(total.astype(BF)))

    layer_out, mix = pl.pallas_call(
        combine_kernel,
        out_shape=[shape((block, width), BF)] * 2,
        in_specs=vmem(3 + chunks),
        out_specs=vmem(2),
        scratch_shapes=[pltpu.VMEM((each, width), BF)],
        compiler_params=params(16),
        name="combine",
    )(hidden, ids, gates, *returned)
    return layer_out[None], mix[None]


def solution(mesh):
    return jax.shard_map(
        per_device,
        mesh=mesh,
        in_specs=(
            P("expert", None, "dp"),
            P("expert", None, "dp"),
            P("expert", None, None),
            P("expert", None, None),
            P("expert", "dp", None, None),
            P("expert", "dp", None),
            P("expert", None),
            P("expert"),
            P("expert", None, None),
            P("dp", None, None),
            P("dp", None, None),
            P("dp", None),
            P(),
            P("expert", "dp", None, None),
            P("expert", "dp", None),
            P("expert", None, None),
            P("expert", None, None),
        ),
        out_specs=(P("expert", "dp", None), P("expert", "dp", None)),
        check_vma=False,
    )
```

```python
import jax
import jax.numpy as jnp
from jax import lax
from jax.experimental import pallas as pl
from jax.experimental.pallas import tpu as pltpu
from jax.sharding import PartitionSpec as P

HD = 128
RD = 64
LAT = 512
TOP = 6
PAGE = 64
EPS = 1e-06
NEG = -1e30

PIECES = 8
SLOTS = 3
SOME = 32
BLOCK = SOME * PIECES
BF = jnp.bfloat16
F32 = jnp.float32


def mm(a, b):
    return jnp.dot(a, b, preferred_element_type=F32)


def mm_nt(a, b):
    return lax.dot_general(a, b, (((1,), (1,)), ((), ())), preferred_element_type=F32)


def mm_tn(a, b):
    return lax.dot_general(a, b, (((0,), (0,)), ((), ())), preferred_element_type=F32)


def vmem(n):
    return [pl.BlockSpec(memory_space=pltpu.VMEM) for _ in range(n)]


def anywhere(n):
    return [pl.BlockSpec(memory_space=pl.ANY) for _ in range(n)]


def start_all(sources, targets, sems):
    copies = [
        pltpu.make_async_copy(a, b, sems.at[i]) for i, (a, b) in enumerate(zip(sources, targets))
    ]
    for copy in copies:
        copy.start()
    return copies


def params(mib):
    return pltpu.CompilerParams(vmem_limit_bytes=mib * 2**20)


def split_kernel(pairs, out):
    out[0] = pairs[0, :, 0, :]
    out[1] = pairs[0, :, 1, :]


def attend_kernel(facts, *refs):
    given, out, (q_scr, ho_scr), held, sems = refs[:11], refs[11], refs[12:14], refs[14:25], refs[25]
    copies = start_all(given, held, sems)
    qn, ku, qr, ln, kr, k0, k1, k2, k3, vu, ow = held
    tokens = qn.shape[0]
    heads = ku.shape[0]
    width = q_scr.shape[1]
    span = k0.shape[0]
    pages = facts.shape[0] - 2
    here = span // PAGE
    for copy in copies[:3]:
        copy.wait()
    for h in range(heads):
        rows = pl.ds(h * tokens, tokens)
        q_scr[rows, 0:LAT] = mm(qn[:, h * HD : (h + 1) * HD], ku[h]).astype(BF)
        rope = qr[:, h * RD : (h + 1) * RD]
        q_scr[rows, LAT:width] = jnp.concatenate(
            [rope, jnp.zeros((tokens, width - LAT - RD), BF)], axis=1
        )
    keys = (k0, k1, k2, k3)
    lane = lax.broadcasted_iota(jnp.int32, (1, span), 1)
    bias = []
    for hop in (0, len(keys) - 1, 1, 2):
        holder = lax.rem(facts[pages + 1] + hop, len(keys))
        first = jnp.zeros((1, span), jnp.int32)
        for i in range(here):
            place = 0
            for j in range(pages):
                place = place + jnp.where(facts[j] == holder * here + i, j, 0)
            first = jnp.where(lane // PAGE == i, place * PAGE, first)
        bias.append(jnp.where(first + lax.rem(lane, PAGE) < facts[pages], 0.0, NEG))
    scale = 1.0 / (HD + RD) ** 0.5
    step = 2
    for h0 in range(0, heads, step):
        n = step * tokens
        q = q_scr[pl.ds(h0 * tokens, n), :]
        row = lax.rem(lax.broadcasted_iota(jnp.int32, (n, tokens), 0), tokens)
        col = lax.broadcasted_iota(jnp.int32, (n, tokens), 1)
        if h0 == 0:
            for copy in copies[3:9]:
                copy.wait()
        s_new = mm_nt(q[:, 0:LAT], ln[...]) + mm(q[:, LAT : LAT + RD], kr[...])
        s_new = jnp.where(col <= row, s_new * scale, NEG)
        s_old = [mm_nt(q, k[...]) * scale + b for k, b in zip(keys, bias)]
        peak = jnp.max(s_new, axis=1, keepdims=True)
        for s in s_old:
            peak = jnp.maximum(peak, jnp.max(s, axis=1, keepdims=True))
        e = jnp.exp(s_new - peak)
        total = jnp.sum(e, axis=1, keepdims=True)
        acc = mm(e.astype(BF), ln[...])
        for s, k in zip(s_old, keys):
            e = jnp.exp(s - peak)
            total = total + jnp.sum(e, axis=1, keepdims=True)
            acc = acc + mm(e.astype(BF), k[:, 0:LAT])
        latent = (acc / total).astype(BF)
        if h0 == 0:
            copies[9].wait()
        for i in range(step):
            ho_scr[:, (h0 + i) * HD : (h0 + i + 1) * HD] = mm(
                latent[i * tokens : (i + 1) * tokens], vu[h0 + i]
            ).astype(BF)
    copies[10].wait()
    for c in range(0, out.shape[1], 512):
        out[:, c : c + 512] = mm(ho_scr[...], ow[:, c : c + 512]).astype(BF)


def count_named(ids, experts):
    block = ids.shape[1]
    expert = lax.broadcasted_iota(jnp.int32, (experts, block), 0)
    named = jnp.zeros((experts, block), F32)
    for k in range(TOP):
        named = named + (ids[k : k + 1, :] == expert).astype(F32)
    a = lax.broadcasted_iota(jnp.int32, (block, block), 0)
    b = lax.broadcasted_iota(jnp.int32, (block, block), 1)
    rank = mm(named.astype(BF), (a < b).astype(BF))
    return jnp.where(named > 0, rank, -1.0)


def by_row(values, total):
    experts = values.shape[0]
    r = lax.broadcasted_iota(jnp.int32, (total, experts), 0)
    c = lax.broadcasted_iota(jnp.int32, (total, experts), 1)
    return mm((r // SLOTS == c).astype(BF), values.astype(BF))


def in_slot(rank_rows, chunk):
    slot = lax.rem(lax.broadcasted_iota(jnp.int32, rank_rows.shape, 0), SLOTS) + chunk * SLOTS
    return rank_rows == slot.astype(F32)


def reorder(transposed):
    i = lax.broadcasted_iota(jnp.int32, (BLOCK, BLOCK), 1 if transposed else 0)
    j = lax.broadcasted_iota(jnp.int32, (BLOCK, BLOCK), 0 if transposed else 1)
    return (j == lax.rem(i, SOME) * PIECES + i // SOME).astype(BF)


def unpack_rows(there, x, rows, base):
    w = x.shape[1]
    for b in range(x.shape[0] // BLOCK):
        out = mm(there, x[b * BLOCK : (b + 1) * BLOCK, :]).astype(BF)
        for p in range(PIECES):
            rows[pl.ds(base + b * SOME, SOME), p * w : (p + 1) * w] = out[
                p * SOME : (p + 1) * SOME
            ]


def pack_rows(back, rows, base, y):
    w = y.shape[1]
    for b in range(y.shape[0] // BLOCK):
        stacked = jnp.concatenate(
            [
                rows[pl.ds(base + b * SOME, SOME), p * w : (p + 1) * w].astype(BF)
                for p in range(PIECES)
            ],
            axis=0,
        )
        y[b * BLOCK : (b + 1) * BLOCK, :] = mm(back, stacked).astype(BF)


def pack_kernel(partial, residual, gain, ids, unused_a, unused_b, hidden_out, *rest):
    chunks = (len(rest) - 3) // 2
    outgoing, (hidden, rows), staged, sems = (
        rest[:chunks],
        rest[chunks : chunks + 2],
        rest[chunks + 2 : -1],
        rest[-1],
    )
    experts = rows.shape[0] // SLOTS
    attended = partial[0].astype(F32)
    for i in range(1, partial.shape[0]):
        attended = attended + partial[i].astype(F32)
    total = residual[...].astype(F32) + attended
    hidden[...] = total
    power = jnp.mean(total * total, axis=1, keepdims=True)
    normed = (total * lax.rsqrt(power + EPS) * gain[...]).astype(BF)
    rank_rows = by_row(count_named(ids, experts), experts * SLOTS)
    back = reorder(True)
    copies = []
    for i, (out, stage) in enumerate(zip(outgoing, staged)):
        rows[...] = mm(in_slot(rank_rows, i).astype(BF), normed).astype(BF)
        pack_rows(back, rows, 0, stage)
        copies.append(pltpu.make_async_copy(stage, out, sems.at[i]))
        copies[-1].start()
    copies.append(pltpu.make_async_copy(hidden, hidden_out, sems.at[chunks]))
    copies[-1].start()
    for copy in copies:
        copy.wait()


def hidden_units(x, w):
    n = w.shape[0] // 2
    gate = mm_nt(x, w[0:n, :])
    up = mm_nt(x, w[n : 2 * n, :])
    return (gate / (1.0 + jnp.exp(-gate)) * up).astype(BF)


def near_kernel(*refs):
    given, results, held = refs[:10], refs[10:12], refs[12:22]
    yl, yr, rows, acc, sems = refs[22:]
    copies = start_all(given, held, sems)
    xl, xr, ia, da, ib, db, fia, fda, fib, fdb = held
    each = rows.shape[0] // 2
    there, back = reorder(False), reorder(True)
    for i, x in enumerate((xl, xr)):
        copies[i].wait()
        unpack_rows(there, x, rows, i * each)
    for copy in copies[2:4]:
        copy.wait()
    acc[...] = mm(hidden_units(rows[...], ia), da[...])
    for copy in copies[4:6]:
        copy.wait()
    acc[...] += mm(hidden_units(rows[...], ib), db[...])
    sent = []
    for i, (fi, fd, y) in enumerate(((fia, fda, yl), (fib, fdb, yr))):
        for copy in copies[6 + 2 * i : 8 + 2 * i]:
            copy.wait()
        part = pl.ds(i * each, each)
        acc[part, :] += mm(hidden_units(rows[part, :], fi), fd[...])
        pack_rows(back, acc, i * each, y)
        sent.append(pltpu.make_async_copy(y, results[i], sems.at[10 + i]))
        sent[-1].start()
    for copy in sent:
        copy.wait()


def own_kernel(x_in, ia_in, da_in, ib_in, db_in, y, x, ia, da, ib, db, rows, acc, sems):
    copies = start_all((x_in, ia_in, da_in, ib_in, db_in), (x, ia, da, ib, db), sems)
    there, back = reorder(False), reorder(True)
    copies[0].wait()
    unpack_rows(there, x, rows, 0)
    for copy in copies[1:3]:
        copy.wait()
    acc[...] = mm(hidden_units(rows[...], ia), da[...])
    for copy in copies[3:5]:
        copy.wait()
    acc[...] += mm(hidden_units(rows[...], ib), db[...])
    pack_rows(back, acc, 0, y)


def combine_kernel(hidden, ids, gates, *rest):
    returned, (layer_out, mix_out, rows) = rest[:-3], rest[-3:]
    experts = rows.shape[0] // SLOTS
    rank = count_named(ids, experts)
    expert = lax.broadcasted_iota(jnp.int32, rank.shape, 0)
    gate = jnp.zeros(rank.shape, F32)
    for k in range(TOP):
        gate = gate + jnp.where(ids[k : k + 1, :] == expert, gates[k : k + 1, :], 0.0)
    high = gate.astype(BF).astype(F32)
    total = experts * SLOTS
    rank_rows, high_rows, low_rows = by_row(rank, total), by_row(high, total), by_row(gate - high, total)
    there = reorder(False)
    mixed = None
    for i, r in enumerate(returned):
        unpack_rows(there, r, rows, 0)
        here = in_slot(rank_rows, i)
        for factor in (high_rows, low_rows):
            term = mm_tn(jnp.where(here, factor, 0.0).astype(BF), rows[...])
            mixed = term if mixed is None else mixed + term
    mix_out[...] = mixed.astype(BF)
    layer_out[...] = (hidden[...] + mixed).astype(BF)


def per_device(
    query_nope,
    query_rope,
    latent_new,
    key_rope,
    latent_pages,
    rope_pages,
    page_table,
    prefix_lengths,
    residual,
    key_up,
    value_up,
    out_weight,
    norm_gain,
    expert_in,
    expert_down,
    expert_ids,
    expert_weights,
):
    groups = lax.axis_size("dp")
    experts = lax.axis_size("expert")
    me = lax.axis_index("dp")
    tokens, width = residual.shape[1:]
    block = tokens // groups
    span = latent_pages.shape[1] * PAGE
    chunks = TOP // SLOTS
    rows = experts * SLOTS * PIECES
    piece = width // PIECES
    shape = jax.ShapeDtypeStruct

    def shift(x, k):
        return lax.ppermute(x, "dp", [(i, (i + k) % groups) for i in range(groups)])

    pad = LAT // 4 - RD
    keys = jnp.concatenate(
        [
            latent_pages[0].reshape(span, LAT),
            rope_pages[0].reshape(span, RD),
            jnp.zeros((span, pad), BF),
        ],
        axis=1,
    )
    from_left, from_right, from_far = shift(keys, 1), shift(keys, -1), shift(keys, 2)

    facts = jnp.concatenate([page_table[0], prefix_lengths, me.astype(jnp.int32)[None]])

    start = me * block
    ids = lax.dynamic_slice_in_dim(expert_ids[0], start, block, 0)
    gates = lax.dynamic_slice_in_dim(expert_weights[0], start, block, 0)
    residual_mine = lax.dynamic_slice_in_dim(residual[0], start, block, 0)
    ids, gates = ids.T, gates.T

    half = expert_in.shape[1] // 2

    some = 16

    def halves(i):
        rows_in = pl.pallas_call(
            split_kernel,
            grid=(half // some,),
            out_shape=shape((2, half, width), BF),
            in_specs=[
                pl.BlockSpec(
                    (1, some, 2, width), lambda j: (0, i * (half // some) + j, 0, 0)
                )
            ],
            out_specs=pl.BlockSpec((2, some, width), lambda j: (0, j, 0)),
            compiler_params=params(56),
            name="split_rows",
        )(expert_in)
        return rows_in.reshape(2 * half, width), expert_down[0, i * half : (i + 1) * half, :]

    (ia, da), (ib, db) = halves(0), halves(1)
    send_da, send_db, from_far = lax.optimization_barrier((da, db, from_far))
    far_da, far_db = shift(send_da, -1), shift(send_db, 1)

    given = (
        query_nope[0],
        key_up,
        query_rope[0],
        latent_new[0],
        key_rope[0].T,
        keys,
        from_left,
        from_right,
        from_far,
        value_up,
        out_weight,
    )
    partial = pl.pallas_call(
        attend_kernel,
        out_shape=shape((tokens, width), BF),
        in_specs=[pl.BlockSpec(memory_space=pltpu.SMEM)] + anywhere(len(given)),
        out_specs=vmem(1)[0],
        scratch_shapes=[
            pltpu.VMEM((key_up.shape[0] * tokens, keys.shape[1]), BF),
            pltpu.VMEM((tokens, key_up.shape[0] * HD), BF),
        ]
        + [pltpu.VMEM(x.shape, BF) for x in given]
        + [pltpu.SemaphoreType.DMA((len(given),))],
        compiler_params=params(56),
        name="attend",
    )(facts, *given)
    partial = lax.all_to_all(
        partial.reshape(groups, block, width), "dp", split_axis=0, concat_axis=0, tiled=True
    )
    send_ia, send_ib, partial = lax.optimization_barrier((ia, ib, partial))
    far_ia, far_ib = shift(send_ia, -1), shift(send_ib, 1)
    hidden, *outgoing = pl.pallas_call(
        pack_kernel,
        out_shape=[shape((block, width), F32)] + [shape((rows, piece), BF)] * chunks,
        in_specs=vmem(4) + anywhere(2),
        out_specs=anywhere(1 + chunks),
        scratch_shapes=[pltpu.VMEM((block, width), F32), pltpu.VMEM((SLOTS * experts, width), BF)]
        + [pltpu.VMEM((rows, piece), BF)] * chunks
        + [pltpu.SemaphoreType.DMA((chunks + 1,))],
        compiler_params=params(56),
        name="pack",
    )(partial, residual_mine, norm_gain.reshape(1, width), ids, far_da, far_db)

    def swap(x):
        x = x.reshape(experts, SLOTS * PIECES, piece)
        x = lax.all_to_all(x, "expert", split_axis=0, concat_axis=0, tiled=True)
        return x.reshape(rows, piece)

    each = SLOTS * experts

    travelling = pltpu.VMEM((rows, piece), BF)
    weights = [pltpu.VMEM(ia.shape, BF), pltpu.VMEM(da.shape, BF)]

    def worked_on(n):
        return [pltpu.VMEM((n * each, width), BF), pltpu.VMEM((n * each, width), F32)]

    near = pl.pallas_call(
        near_kernel,
        out_shape=[shape((rows, piece), BF)] * 2,
        in_specs=anywhere(10),
        out_specs=anywhere(2),
        scratch_shapes=[travelling] * 2
        + weights * 4
        + [travelling] * 2
        + worked_on(2)
        + [pltpu.SemaphoreType.DMA((12,))],
        compiler_params=params(56),
        name="near_experts",
    )
    own = pl.pallas_call(
        own_kernel,
        out_shape=shape((rows, piece), BF),
        in_specs=anywhere(5),
        out_specs=vmem(1)[0],
        scratch_shapes=[travelling]
        + weights * 2
        + worked_on(1)
        + [pltpu.SemaphoreType.DMA((5,))],
        compiler_params=params(56),
        name="own_experts",
    )
    arrived = [swap(x) for x in outgoing]
    returned = []
    for x in arrived:
        left, right = near(
            shift(x, 1), shift(x, -1), ia, da, ib, db, far_ia, far_da, far_ib, far_db
        )
        mine = own(x, ia, da, ib, db)
        total = mine.astype(F32) + shift(left, -1).astype(F32) + shift(right, 1).astype(F32)
        returned.append(swap(total.astype(BF)))

    layer_out, mix = pl.pallas_call(
        combine_kernel,
        out_shape=[shape((block, width), BF)] * 2,
        in_specs=vmem(3 + chunks),
        out_specs=vmem(2),
        scratch_shapes=[pltpu.VMEM((each, width), BF)],
        compiler_params=params(56),
        name="combine",
    )(hidden, ids, gates, *returned)
    return layer_out[None], mix[None]


def solution(mesh):
    return jax.shard_map(
        per_device,
        mesh=mesh,
        in_specs=(
            P("expert", None, "dp"),
            P("expert", None, "dp"),
            P("expert", None, None),
            P("expert", None, None),
            P("expert", "dp", None, None),
            P("expert", "dp", None),
            P("expert", None),
            P("expert"),
            P("expert", None, None),
            P("dp", None, None),
            P("dp", None, None),
            P("dp", None),
            P(),
            P("expert", "dp", None, None),
            P("expert", "dp", None),
            P("expert", None, None),
            P("expert", None, None),
        ),
        out_specs=(P("expert", "dp", None), P("expert", "dp", None)),
        check_vma=False,
    )
```

```python
import jax
import jax.numpy as jnp
from jax import lax
from jax.experimental import pallas as pl
from jax.experimental.pallas import tpu as pltpu
from jax.sharding import PartitionSpec as P

HD = 128
RD = 64
LAT = 512
TOP = 6
PAGE = 64
EPS = 1e-06
NEG = -1e30

PIECES = 8
SLOTS = 3
SOME = 32
BLOCK = SOME * PIECES
BF = jnp.bfloat16
F32 = jnp.float32


def mm(a, b):
    return jnp.dot(a, b, preferred_element_type=F32)


def mm_nt(a, b):
    return lax.dot_general(a, b, (((1,), (1,)), ((), ())), preferred_element_type=F32)


def mm_tn(a, b):
    return lax.dot_general(a, b, (((0,), (0,)), ((), ())), preferred_element_type=F32)


def vmem(n):
    return [pl.BlockSpec(memory_space=pltpu.VMEM) for _ in range(n)]


def anywhere(n):
    return [pl.BlockSpec(memory_space=pl.ANY) for _ in range(n)]


def start_all(sources, targets, sems):
    copies = [
        pltpu.make_async_copy(a, b, sems.at[i]) for i, (a, b) in enumerate(zip(sources, targets))
    ]
    for copy in copies:
        copy.start()
    return copies


def params(mib):
    return pltpu.CompilerParams(vmem_limit_bytes=mib * 2**20)


def split_kernel(pairs, out):
    out[0] = pairs[0, :, 0, :]
    out[1] = pairs[0, :, 1, :]


def attend_kernel(facts, *refs):
    given, out, (q_scr, ho_scr), held, sems = refs[:11], refs[11], refs[12:14], refs[14:25], refs[25]
    copies = start_all(given, held, sems)
    qn, ku, qr, ln, kr, k0, k1, k2, k3, vu, ow = held
    tokens = qn.shape[0]
    heads = ku.shape[0]
    width = q_scr.shape[1]
    span = k0.shape[0]
    pages = facts.shape[0] - 2
    here = span // PAGE
    for copy in copies[:3]:
        copy.wait()
    for h in range(heads):
        rows = pl.ds(h * tokens, tokens)
        q_scr[rows, 0:LAT] = mm(qn[:, h * HD : (h + 1) * HD], ku[h]).astype(BF)
        rope = qr[:, h * RD : (h + 1) * RD]
        q_scr[rows, LAT:width] = jnp.concatenate(
            [rope, jnp.zeros((tokens, width - LAT - RD), BF)], axis=1
        )
    keys = (k0, k1, k2, k3)
    lane = lax.broadcasted_iota(jnp.int32, (1, span), 1)
    bias = []
    for hop in (0, len(keys) - 1, 1, 2):
        holder = lax.rem(facts[pages + 1] + hop, len(keys))
        first = jnp.zeros((1, span), jnp.int32)
        for i in range(here):
            place = 0
            for j in range(pages):
                place = place + jnp.where(facts[j] == holder * here + i, j, 0)
            first = jnp.where(lane // PAGE == i, place * PAGE, first)
        bias.append(jnp.where(first + lax.rem(lane, PAGE) < facts[pages], 0.0, NEG))
    scale = 1.0 / (HD + RD) ** 0.5
    step = 2
    for h0 in range(0, heads, step):
        n = step * tokens
        q = q_scr[pl.ds(h0 * tokens, n), :]
        row = lax.rem(lax.broadcasted_iota(jnp.int32, (n, tokens), 0), tokens)
        col = lax.broadcasted_iota(jnp.int32, (n, tokens), 1)
        if h0 == 0:
            for copy in copies[3:9]:
                copy.wait()
        s_new = mm_nt(q[:, 0:LAT], ln[...]) + mm(q[:, LAT : LAT + RD], kr[...])
        s_new = jnp.where(col <= row, s_new * scale, NEG)
        s_old = [mm_nt(q, k[...]) * scale + b for k, b in zip(keys, bias)]
        peak = jnp.max(s_new, axis=1, keepdims=True)
        for s in s_old:
            peak = jnp.maximum(peak, jnp.max(s, axis=1, keepdims=True))
        e = jnp.exp(s_new - peak)
        total = jnp.sum(e, axis=1, keepdims=True)
        acc = mm(e.astype(BF), ln[...])
        for s, k in zip(s_old, keys):
            e = jnp.exp(s - peak)
            total = total + jnp.sum(e, axis=1, keepdims=True)
            acc = acc + mm(e.astype(BF), k[:, 0:LAT])
        latent = (acc / total).astype(BF)
        if h0 == 0:
            copies[9].wait()
        for i in range(step):
            ho_scr[:, (h0 + i) * HD : (h0 + i + 1) * HD] = mm(
                latent[i * tokens : (i + 1) * tokens], vu[h0 + i]
            ).astype(BF)
    copies[10].wait()
    for c in range(0, out.shape[1], 512):
        out[:, c : c + 512] = mm(ho_scr[...], ow[:, c : c + 512]).astype(BF)


def count_named(ids, experts):
    block = ids.shape[1]
    expert = lax.broadcasted_iota(jnp.int32, (experts, block), 0)
    named = jnp.zeros((experts, block), F32)
    for k in range(TOP):
        named = named + (ids[k : k + 1, :] == expert).astype(F32)
    a = lax.broadcasted_iota(jnp.int32, (block, block), 0)
    b = lax.broadcasted_iota(jnp.int32, (block, block), 1)
    rank = mm(named.astype(BF), (a < b).astype(BF))
    return jnp.where(named > 0, rank, -1.0)


def by_row(values, total):
    experts = values.shape[0]
    r = lax.broadcasted_iota(jnp.int32, (total, experts), 0)
    c = lax.broadcasted_iota(jnp.int32, (total, experts), 1)
    return mm((r // SLOTS == c).astype(BF), values.astype(BF))


def in_slot(rank_rows, chunk):
    slot = lax.rem(lax.broadcasted_iota(jnp.int32, rank_rows.shape, 0), SLOTS) + chunk * SLOTS
    return rank_rows == slot.astype(F32)


def reorder(transposed):
    i = lax.broadcasted_iota(jnp.int32, (BLOCK, BLOCK), 1 if transposed else 0)
    j = lax.broadcasted_iota(jnp.int32, (BLOCK, BLOCK), 0 if transposed else 1)
    return (j == lax.rem(i, SOME) * PIECES + i // SOME).astype(BF)


def unpack_rows(there, x, rows, base):
    w = x.shape[1]
    for b in range(x.shape[0] // BLOCK):
        out = mm(there, x[b * BLOCK : (b + 1) * BLOCK, :]).astype(BF)
        for p in range(PIECES):
            rows[pl.ds(base + b * SOME, SOME), p * w : (p + 1) * w] = out[
                p * SOME : (p + 1) * SOME
            ]


def pack_rows(back, rows, base, y):
    w = y.shape[1]
    for b in range(y.shape[0] // BLOCK):
        stacked = jnp.concatenate(
            [
                rows[pl.ds(base + b * SOME, SOME), p * w : (p + 1) * w].astype(BF)
                for p in range(PIECES)
            ],
            axis=0,
        )
        y[b * BLOCK : (b + 1) * BLOCK, :] = mm(back, stacked).astype(BF)


def pack_kernel(partial, residual, gain, ids, unused_a, unused_b, hidden_out, *rest):
    chunks = (len(rest) - 3) // 2
    outgoing, (hidden, rows), staged, sems = (
        rest[:chunks],
        rest[chunks : chunks + 2],
        rest[chunks + 2 : -1],
        rest[-1],
    )
    experts = rows.shape[0] // SLOTS
    attended = partial[0].astype(F32)
    for i in range(1, partial.shape[0]):
        attended = attended + partial[i].astype(F32)
    total = residual[...].astype(F32) + attended
    hidden[...] = total
    power = jnp.mean(total * total, axis=1, keepdims=True)
    normed = (total * lax.rsqrt(power + EPS) * gain[...]).astype(BF)
    rank_rows = by_row(count_named(ids, experts), experts * SLOTS)
    back = reorder(True)
    copies = []
    for i, (out, stage) in enumerate(zip(outgoing, staged)):
        rows[...] = mm(in_slot(rank_rows, i).astype(BF), normed).astype(BF)
        pack_rows(back, rows, 0, stage)
        copies.append(pltpu.make_async_copy(stage, out, sems.at[i]))
        copies[-1].start()
    copies.append(pltpu.make_async_copy(hidden, hidden_out, sems.at[chunks]))
    copies[-1].start()
    for copy in copies:
        copy.wait()


def hidden_units(x, w):
    n = w.shape[0] // 2
    gate = mm_nt(x, w[0:n, :])
    up = mm_nt(x, w[n : 2 * n, :])
    return (gate / (1.0 + jnp.exp(-gate)) * up).astype(BF)


def near_kernel(*refs):
    given, results, held = refs[:10], refs[10:12], refs[12:22]
    yl, yr, rows, acc, sems = refs[22:]
    copies = start_all(given, held, sems)
    xl, xr, ia, da, ib, db, fia, fda, fib, fdb = held
    each = rows.shape[0] // 2
    there, back = reorder(False), reorder(True)
    for i, x in enumerate((xl, xr)):
        copies[i].wait()
        unpack_rows(there, x, rows, i * each)
    for copy in copies[2:4]:
        copy.wait()
    acc[...] = mm(hidden_units(rows[...], ia), da[...])
    for copy in copies[4:6]:
        copy.wait()
    acc[...] += mm(hidden_units(rows[...], ib), db[...])
    sent = []
    for i, (fi, fd, y) in enumerate(((fia, fda, yl), (fib, fdb, yr))):
        for copy in copies[6 + 2 * i : 8 + 2 * i]:
            copy.wait()
        part = pl.ds(i * each, each)
        acc[part, :] += mm(hidden_units(rows[part, :], fi), fd[...])
        pack_rows(back, acc, i * each, y)
        sent.append(pltpu.make_async_copy(y, results[i], sems.at[10 + i]))
        sent[-1].start()
    for copy in sent:
        copy.wait()


def own_kernel(x_in, ia_in, da_in, ib_in, db_in, y, x, ia, da, ib, db, rows, acc, sems):
    copies = start_all((x_in, ia_in, da_in, ib_in, db_in), (x, ia, da, ib, db), sems)
    there, back = reorder(False), reorder(True)
    copies[0].wait()
    unpack_rows(there, x, rows, 0)
    for copy in copies[1:3]:
        copy.wait()
    acc[...] = mm(hidden_units(rows[...], ia), da[...])
    for copy in copies[3:5]:
        copy.wait()
    acc[...] += mm(hidden_units(rows[...], ib), db[...])
    pack_rows(back, acc, 0, y)


def combine_kernel(hidden, ids, gates, *rest):
    returned, (layer_out, mix_out, rows) = rest[:-3], rest[-3:]
    experts = rows.shape[0] // SLOTS
    rank = count_named(ids, experts)
    expert = lax.broadcasted_iota(jnp.int32, rank.shape, 0)
    gate = jnp.zeros(rank.shape, F32)
    for k in range(TOP):
        gate = gate + jnp.where(ids[k : k + 1, :] == expert, gates[k : k + 1, :], 0.0)
    high = gate.astype(BF).astype(F32)
    total = experts * SLOTS
    rank_rows, high_rows, low_rows = by_row(rank, total), by_row(high, total), by_row(gate - high, total)
    there = reorder(False)
    mixed = None
    for i, r in enumerate(returned):
        unpack_rows(there, r, rows, 0)
        here = in_slot(rank_rows, i)
        for factor in (high_rows, low_rows):
            term = mm_tn(jnp.where(here, factor, 0.0).astype(BF), rows[...])
            mixed = term if mixed is None else mixed + term
    mix_out[...] = mixed.astype(BF)
    layer_out[...] = (hidden[...] + mixed).astype(BF)


def per_device(
    query_nope,
    query_rope,
    latent_new,
    key_rope,
    latent_pages,
    rope_pages,
    page_table,
    prefix_lengths,
    residual,
    key_up,
    value_up,
    out_weight,
    norm_gain,
    expert_in,
    expert_down,
    expert_ids,
    expert_weights,
):
    groups = lax.axis_size("dp")
    experts = lax.axis_size("expert")
    me = lax.axis_index("dp")
    tokens, width = residual.shape[1:]
    block = tokens // groups
    span = latent_pages.shape[1] * PAGE
    chunks = TOP // SLOTS
    rows = experts * SLOTS * PIECES
    piece = width // PIECES
    shape = jax.ShapeDtypeStruct

    def shift(x, k):
        return lax.ppermute(x, "dp", [(i, (i + k) % groups) for i in range(groups)])

    pad = LAT // 4 - RD
    keys = jnp.concatenate(
        [
            latent_pages[0].reshape(span, LAT),
            rope_pages[0].reshape(span, RD),
            jnp.zeros((span, pad), BF),
        ],
        axis=1,
    )
    from_left, from_right, from_far = shift(keys, 1), shift(keys, -1), shift(keys, 2)

    facts = jnp.concatenate([page_table[0], prefix_lengths, me.astype(jnp.int32)[None]])

    start = me * block
    ids = lax.dynamic_slice_in_dim(expert_ids[0], start, block, 0)
    gates = lax.dynamic_slice_in_dim(expert_weights[0], start, block, 0)
    residual_mine = lax.dynamic_slice_in_dim(residual[0], start, block, 0)
    ids, gates = ids.T, gates.T

    half = expert_in.shape[1] // 2

    def split_half(x, i):
        rows_in = pl.pallas_call(
            split_kernel,
            grid=(1,),
            out_shape=shape((2, half, width), BF),
            in_specs=[pl.BlockSpec((1, half, 2, width), lambda j: (0, i, 0, 0))],
            out_specs=pl.BlockSpec((2, half, width), lambda j: (0, 0, 0)),
            compiler_params=params(56),
            name="split_rows",
        )(x)
        return rows_in.reshape(2 * half, width)

    ia = split_half(expert_in, 0)
    da, db = expert_down[0, :half, :], expert_down[0, half:, :]
    send_da, send_db, ia, from_far = lax.optimization_barrier((da, db, ia, from_far))
    far_da, far_db = shift(send_da, -1), shift(send_db, 1)

    given = (
        query_nope[0],
        key_up,
        query_rope[0],
        latent_new[0],
        key_rope[0].T,
        keys,
        from_left,
        from_right,
        from_far,
        value_up,
        out_weight,
    )
    partial = pl.pallas_call(
        attend_kernel,
        out_shape=shape((tokens, width), BF),
        in_specs=[pl.BlockSpec(memory_space=pltpu.SMEM)] + anywhere(len(given)),
        out_specs=vmem(1)[0],
        scratch_shapes=[
            pltpu.VMEM((key_up.shape[0] * tokens, keys.shape[1]), BF),
            pltpu.VMEM((tokens, key_up.shape[0] * HD), BF),
        ]
        + [pltpu.VMEM(x.shape, BF) for x in given]
        + [pltpu.SemaphoreType.DMA((len(given),))],
        compiler_params=params(56),
        name="attend",
    )(facts, *given)
    later_in, partial = lax.optimization_barrier((expert_in, partial))
    ib = split_half(later_in, 1)
    partial = lax.all_to_all(
        partial.reshape(groups, block, width), "dp", split_axis=0, concat_axis=0, tiled=True
    )
    send_ia, send_ib, partial = lax.optimization_barrier((ia, ib, partial))
    far_ia, far_ib = shift(send_ia, -1), shift(send_ib, 1)
    hidden, *outgoing = pl.pallas_call(
        pack_kernel,
        out_shape=[shape((block, width), F32)] + [shape((rows, piece), BF)] * chunks,
        in_specs=vmem(4) + anywhere(2),
        out_specs=anywhere(1 + chunks),
        scratch_shapes=[pltpu.VMEM((block, width), F32), pltpu.VMEM((SLOTS * experts, width), BF)]
        + [pltpu.VMEM((rows, piece), BF)] * chunks
        + [pltpu.SemaphoreType.DMA((chunks + 1,))],
        compiler_params=params(56),
        name="pack",
    )(partial, residual_mine, norm_gain.reshape(1, width), ids, far_da, far_db)

    def swap(x):
        x = x.reshape(experts, SLOTS * PIECES, piece)
        x = lax.all_to_all(x, "expert", split_axis=0, concat_axis=0, tiled=True)
        return x.reshape(rows, piece)

    each = SLOTS * experts

    travelling = pltpu.VMEM((rows, piece), BF)
    weights = [pltpu.VMEM(ia.shape, BF), pltpu.VMEM(da.shape, BF)]

    def worked_on(n):
        return [pltpu.VMEM((n * each, width), BF), pltpu.VMEM((n * each, width), F32)]

    near = pl.pallas_call(
        near_kernel,
        out_shape=[shape((rows, piece), BF)] * 2,
        in_specs=anywhere(10),
        out_specs=anywhere(2),
        scratch_shapes=[travelling] * 2
        + weights * 4
        + [travelling] * 2
        + worked_on(2)
        + [pltpu.SemaphoreType.DMA((12,))],
        compiler_params=params(56),
        name="near_experts",
    )
    own = pl.pallas_call(
        own_kernel,
        out_shape=shape((rows, piece), BF),
        in_specs=anywhere(5),
        out_specs=vmem(1)[0],
        scratch_shapes=[travelling]
        + weights * 2
        + worked_on(1)
        + [pltpu.SemaphoreType.DMA((5,))],
        compiler_params=params(56),
        name="own_experts",
    )
    arrived = [swap(x) for x in outgoing]
    returned = []
    for x in arrived:
        left, right = near(
            shift(x, 1), shift(x, -1), ia, da, ib, db, far_ia, far_da, far_ib, far_db
        )
        mine = own(x, ia, da, ib, db)
        total = mine.astype(F32) + shift(left, -1).astype(F32) + shift(right, 1).astype(F32)
        returned.append(swap(total.astype(BF)))

    layer_out, mix = pl.pallas_call(
        combine_kernel,
        out_shape=[shape((block, width), BF)] * 2,
        in_specs=vmem(3 + chunks),
        out_specs=vmem(2),
        scratch_shapes=[pltpu.VMEM((each, width), BF)],
        compiler_params=params(56),
        name="combine",
    )(hidden, ids, gates, *returned)
    return layer_out[None], mix[None]


def solution(mesh):
    return jax.shard_map(
        per_device,
        mesh=mesh,
        in_specs=(
            P("expert", None, "dp"),
            P("expert", None, "dp"),
            P("expert", None, None),
            P("expert", None, None),
            P("expert", "dp", None, None),
            P("expert", "dp", None),
            P("expert", None),
            P("expert"),
            P("expert", None, None),
            P("dp", None, None),
            P("dp", None, None),
            P("dp", None),
            P(),
            P("expert", "dp", None, None),
            P("expert", "dp", None),
            P("expert", None, None),
            P("expert", None, None),
        ),
        out_specs=(P("expert", "dp", None), P("expert", "dp", None)),
        check_vma=False,
    )
```

```python
import jax
import jax.numpy as jnp
from jax import lax
from jax.experimental import pallas as pl
from jax.experimental.pallas import tpu as pltpu
from jax.sharding import PartitionSpec as P

HD = 128
RD = 64
LAT = 512
TOP = 6
PAGE = 64
EPS = 1e-06
NEG = -1e30

PIECES = 8
SLOTS = 3
SOME = 32
BLOCK = SOME * PIECES
BF = jnp.bfloat16
F32 = jnp.float32


def mm(a, b):
    return jnp.dot(a, b, preferred_element_type=F32)


def mm_nt(a, b):
    return lax.dot_general(a, b, (((1,), (1,)), ((), ())), preferred_element_type=F32)


def mm_tn(a, b):
    return lax.dot_general(a, b, (((0,), (0,)), ((), ())), preferred_element_type=F32)


def vmem(n):
    return [pl.BlockSpec(memory_space=pltpu.VMEM) for _ in range(n)]


def anywhere(n):
    return [pl.BlockSpec(memory_space=pl.ANY) for _ in range(n)]


def start_all(sources, targets, sems):
    copies = [
        pltpu.make_async_copy(a, b, sems.at[i]) for i, (a, b) in enumerate(zip(sources, targets))
    ]
    for copy in copies:
        copy.start()
    return copies


def params(mib):
    return pltpu.CompilerParams(vmem_limit_bytes=mib * 2**20)


def split_kernel(pairs, out):
    out[0] = pairs[0, :, 0, :]
    out[1] = pairs[0, :, 1, :]


def attend_kernel(facts, *refs):
    given, out, (q_scr, ho_scr), held, sems = refs[:11], refs[11], refs[12:14], refs[14:25], refs[25]
    copies = start_all(given, held, sems)
    qn, ku, qr, ln, kr, k0, k1, k2, k3, vu, ow = held
    tokens = qn.shape[0]
    heads = ku.shape[0]
    width = q_scr.shape[1]
    span = k0.shape[0]
    pages = facts.shape[0] - 2
    here = span // PAGE
    for copy in copies[:3]:
        copy.wait()
    for h in range(heads):
        rows = pl.ds(h * tokens, tokens)
        q_scr[rows, 0:LAT] = mm(qn[:, h * HD : (h + 1) * HD], ku[h]).astype(BF)
        rope = qr[:, h * RD : (h + 1) * RD]
        q_scr[rows, LAT:width] = jnp.concatenate(
            [rope, jnp.zeros((tokens, width - LAT - RD), BF)], axis=1
        )
    keys = (k0, k1, k2, k3)
    lane = lax.broadcasted_iota(jnp.int32, (1, span), 1)
    bias = []
    for hop in (0, len(keys) - 1, 1, 2):
        holder = lax.rem(facts[pages + 1] + hop, len(keys))
        first = jnp.zeros((1, span), jnp.int32)
        for i in range(here):
            place = 0
            for j in range(pages):
                place = place + jnp.where(facts[j] == holder * here + i, j, 0)
            first = jnp.where(lane // PAGE == i, place * PAGE, first)
        bias.append(jnp.where(first + lax.rem(lane, PAGE) < facts[pages], 0.0, NEG))
    scale = 1.0 / (HD + RD) ** 0.5
    step = 2
    for h0 in range(0, heads, step):
        n = step * tokens
        q = q_scr[pl.ds(h0 * tokens, n), :]
        row = lax.rem(lax.broadcasted_iota(jnp.int32, (n, tokens), 0), tokens)
        col = lax.broadcasted_iota(jnp.int32, (n, tokens), 1)
        if h0 == 0:
            for copy in copies[3:9]:
                copy.wait()
        s_new = mm_nt(q[:, 0:LAT], ln[...]) + mm(q[:, LAT : LAT + RD], kr[...])
        s_new = jnp.where(col <= row, s_new * scale, NEG)
        s_old = [mm_nt(q, k[...]) * scale + b for k, b in zip(keys, bias)]
        peak = jnp.max(s_new, axis=1, keepdims=True)
        for s in s_old:
            peak = jnp.maximum(peak, jnp.max(s, axis=1, keepdims=True))
        e = jnp.exp(s_new - peak)
        total = jnp.sum(e, axis=1, keepdims=True)
        acc = mm(e.astype(BF), ln[...])
        for s, k in zip(s_old, keys):
            e = jnp.exp(s - peak)
            total = total + jnp.sum(e, axis=1, keepdims=True)
            acc = acc + mm(e.astype(BF), k[:, 0:LAT])
        latent = (acc / total).astype(BF)
        if h0 == 0:
            copies[9].wait()
        for i in range(step):
            ho_scr[:, (h0 + i) * HD : (h0 + i + 1) * HD] = mm(
                latent[i * tokens : (i + 1) * tokens], vu[h0 + i]
            ).astype(BF)
    copies[10].wait()
    for c in range(0, out.shape[1], 512):
        out[:, c : c + 512] = mm(ho_scr[...], ow[:, c : c + 512]).astype(BF)


def count_named(ids, experts):
    block = ids.shape[1]
    expert = lax.broadcasted_iota(jnp.int32, (experts, block), 0)
    named = jnp.zeros((experts, block), F32)
    for k in range(TOP):
        named = named + (ids[k : k + 1, :] == expert).astype(F32)
    a = lax.broadcasted_iota(jnp.int32, (block, block), 0)
    b = lax.broadcasted_iota(jnp.int32, (block, block), 1)
    rank = mm(named.astype(BF), (a < b).astype(BF))
    return jnp.where(named > 0, rank, -1.0)


def by_row(values, total):
    experts = values.shape[0]
    r = lax.broadcasted_iota(jnp.int32, (total, experts), 0)
    c = lax.broadcasted_iota(jnp.int32, (total, experts), 1)
    return mm((r // SLOTS == c).astype(BF), values.astype(BF))


def in_slot(rank_rows, chunk):
    slot = lax.rem(lax.broadcasted_iota(jnp.int32, rank_rows.shape, 0), SLOTS) + chunk * SLOTS
    return rank_rows == slot.astype(F32)


def reorder(transposed):
    i = lax.broadcasted_iota(jnp.int32, (BLOCK, BLOCK), 1 if transposed else 0)
    j = lax.broadcasted_iota(jnp.int32, (BLOCK, BLOCK), 0 if transposed else 1)
    return (j == lax.rem(i, SOME) * PIECES + i // SOME).astype(BF)


def unpack_rows(there, x, rows, base):
    w = x.shape[1]
    for b in range(x.shape[0] // BLOCK):
        out = mm(there, x[b * BLOCK : (b + 1) * BLOCK, :]).astype(BF)
        for p in range(PIECES):
            rows[pl.ds(base + b * SOME, SOME), p * w : (p + 1) * w] = out[
                p * SOME : (p + 1) * SOME
            ]


def pack_rows(back, rows, base, y):
    w = y.shape[1]
    for b in range(y.shape[0] // BLOCK):
        stacked = jnp.concatenate(
            [
                rows[pl.ds(base + b * SOME, SOME), p * w : (p + 1) * w].astype(BF)
                for p in range(PIECES)
            ],
            axis=0,
        )
        y[b * BLOCK : (b + 1) * BLOCK, :] = mm(back, stacked).astype(BF)


def pack_kernel(partial, residual, gain, ids, unused_a, unused_b, hidden_out, *rest):
    chunks = (len(rest) - 3) // 2
    outgoing, (hidden, rows), staged, sems = (
        rest[:chunks],
        rest[chunks : chunks + 2],
        rest[chunks + 2 : -1],
        rest[-1],
    )
    experts = rows.shape[0] // SLOTS
    attended = partial[0].astype(F32)
    for i in range(1, partial.shape[0]):
        attended = attended + partial[i].astype(F32)
    total = residual[...].astype(F32) + attended
    hidden[...] = total
    power = jnp.mean(total * total, axis=1, keepdims=True)
    normed = (total * lax.rsqrt(power + EPS) * gain[...]).astype(BF)
    rank_rows = by_row(count_named(ids, experts), experts * SLOTS)
    back = reorder(True)
    copies = []
    for i, (out, stage) in enumerate(zip(outgoing, staged)):
        rows[...] = mm(in_slot(rank_rows, i).astype(BF), normed).astype(BF)
        pack_rows(back, rows, 0, stage)
        copies.append(pltpu.make_async_copy(stage, out, sems.at[i]))
        copies[-1].start()
    copies.append(pltpu.make_async_copy(hidden, hidden_out, sems.at[chunks]))
    copies[-1].start()
    for copy in copies:
        copy.wait()


def hidden_units(x, w):
    n = w.shape[0] // 2
    gate = mm_nt(x, w[0:n, :])
    up = mm_nt(x, w[n : 2 * n, :])
    return (gate / (1.0 + jnp.exp(-gate)) * up).astype(BF)


def hold_kernel(unused, *refs):
    n = len(refs) // 2
    for copy in start_all(refs[:n], refs[n : 2 * n], refs[-1]):
        copy.wait()


def near_kernel(xl, xr, ia, da, ib, db, fia, fda, fib, fdb, yl, yr, rows, acc):
    each = rows.shape[0] // 2
    there, back = reorder(False), reorder(True)
    for i, x in enumerate((xl, xr)):
        unpack_rows(there, x, rows, i * each)
    acc[...] = mm(hidden_units(rows[...], ia), da[...])
    acc[...] += mm(hidden_units(rows[...], ib), db[...])
    for i, (fi, fd, y) in enumerate(((fia, fda, yl), (fib, fdb, yr))):
        part = pl.ds(i * each, each)
        acc[part, :] += mm(hidden_units(rows[part, :], fi), fd[...])
        pack_rows(back, acc, i * each, y)


def own_kernel(x, ia, da, ib, db, y, rows, acc):
    there, back = reorder(False), reorder(True)
    unpack_rows(there, x, rows, 0)
    acc[...] = mm(hidden_units(rows[...], ia), da[...])
    acc[...] += mm(hidden_units(rows[...], ib), db[...])
    pack_rows(back, acc, 0, y)


def combine_kernel(hidden, ids, gates, *rest):
    returned, (layer_out, mix_out, rows) = rest[:-3], rest[-3:]
    experts = rows.shape[0] // SLOTS
    rank = count_named(ids, experts)
    expert = lax.broadcasted_iota(jnp.int32, rank.shape, 0)
    gate = jnp.zeros(rank.shape, F32)
    for k in range(TOP):
        gate = gate + jnp.where(ids[k : k + 1, :] == expert, gates[k : k + 1, :], 0.0)
    high = gate.astype(BF).astype(F32)
    total = experts * SLOTS
    rank_rows, high_rows, low_rows = by_row(rank, total), by_row(high, total), by_row(gate - high, total)
    there = reorder(False)
    mixed = None
    for i, r in enumerate(returned):
        unpack_rows(there, r, rows, 0)
        here = in_slot(rank_rows, i)
        for factor in (high_rows, low_rows):
            term = mm_tn(jnp.where(here, factor, 0.0).astype(BF), rows[...])
            mixed = term if mixed is None else mixed + term
    mix_out[...] = mixed.astype(BF)
    layer_out[...] = (hidden[...] + mixed).astype(BF)


def per_device(
    query_nope,
    query_rope,
    latent_new,
    key_rope,
    latent_pages,
    rope_pages,
    page_table,
    prefix_lengths,
    residual,
    key_up,
    value_up,
    out_weight,
    norm_gain,
    expert_in,
    expert_down,
    expert_ids,
    expert_weights,
):
    groups = lax.axis_size("dp")
    experts = lax.axis_size("expert")
    me = lax.axis_index("dp")
    tokens, width = residual.shape[1:]
    block = tokens // groups
    span = latent_pages.shape[1] * PAGE
    chunks = TOP // SLOTS
    rows = experts * SLOTS * PIECES
    piece = width // PIECES
    shape = jax.ShapeDtypeStruct

    def shift(x, k):
        return lax.ppermute(x, "dp", [(i, (i + k) % groups) for i in range(groups)])

    pad = LAT // 4 - RD
    keys = jnp.concatenate(
        [
            latent_pages[0].reshape(span, LAT),
            rope_pages[0].reshape(span, RD),
            jnp.zeros((span, pad), BF),
        ],
        axis=1,
    )
    from_left, from_right, from_far = shift(keys, 1), shift(keys, -1), shift(keys, 2)

    facts = jnp.concatenate([page_table[0], prefix_lengths, me.astype(jnp.int32)[None]])

    start = me * block
    ids = lax.dynamic_slice_in_dim(expert_ids[0], start, block, 0)
    gates = lax.dynamic_slice_in_dim(expert_weights[0], start, block, 0)
    residual_mine = lax.dynamic_slice_in_dim(residual[0], start, block, 0)
    ids, gates = ids.T, gates.T

    half = expert_in.shape[1] // 2

    def split_half(x, i):
        rows_in = pl.pallas_call(
            split_kernel,
            grid=(1,),
            out_shape=shape((2, half, width), BF),
            in_specs=[pl.BlockSpec((1, half, 2, width), lambda j: (0, i, 0, 0))],
            out_specs=pl.BlockSpec((2, half, width), lambda j: (0, 0, 0)),
            compiler_params=params(56),
            name="split_rows",
        )(x)
        return rows_in.reshape(2 * half, width)

    ia = split_half(expert_in, 0)
    da, db = expert_down[0, :half, :], expert_down[0, half:, :]
    send_da, send_db, ia, from_far = lax.optimization_barrier((da, db, ia, from_far))
    far_da, far_db = shift(send_da, -1), shift(send_db, 1)

    given = (
        query_nope[0],
        key_up,
        query_rope[0],
        latent_new[0],
        key_rope[0].T,
        keys,
        from_left,
        from_right,
        from_far,
        value_up,
        out_weight,
    )
    partial = pl.pallas_call(
        attend_kernel,
        out_shape=shape((tokens, width), BF),
        in_specs=[pl.BlockSpec(memory_space=pltpu.SMEM)] + anywhere(len(given)),
        out_specs=vmem(1)[0],
        scratch_shapes=[
            pltpu.VMEM((key_up.shape[0] * tokens, keys.shape[1]), BF),
            pltpu.VMEM((tokens, key_up.shape[0] * HD), BF),
        ]
        + [pltpu.VMEM(x.shape, BF) for x in given]
        + [pltpu.SemaphoreType.DMA((len(given),))],
        compiler_params=params(56),
        name="attend",
    )(facts, *given)
    later_in, partial = lax.optimization_barrier((expert_in, partial))
    ib = split_half(later_in, 1)
    partial = lax.all_to_all(
        partial.reshape(groups, block, width), "dp", split_axis=0, concat_axis=0, tiled=True
    )
    send_ia, send_ib, partial = lax.optimization_barrier((ia, ib, partial))
    far_ia, far_ib = shift(send_ia, -1), shift(send_ib, 1)
    hidden, *outgoing = pl.pallas_call(
        pack_kernel,
        out_shape=[shape((block, width), F32)] + [shape((rows, piece), BF)] * chunks,
        in_specs=vmem(4) + anywhere(2),
        out_specs=anywhere(1 + chunks),
        scratch_shapes=[pltpu.VMEM((block, width), F32), pltpu.VMEM((SLOTS * experts, width), BF)]
        + [pltpu.VMEM((rows, piece), BF)] * chunks
        + [pltpu.SemaphoreType.DMA((chunks + 1,))],
        compiler_params=params(56),
        name="pack",
    )(partial, residual_mine, norm_gain.reshape(1, width), ids, far_da, far_db)

    def swap(x):
        x = x.reshape(experts, SLOTS * PIECES, piece)
        x = lax.all_to_all(x, "expert", split_axis=0, concat_axis=0, tiled=True)
        return x.reshape(rows, piece)

    each = SLOTS * experts

    weights = (ia, da, ib, db, far_ia, far_da, far_ib, far_db)
    hold = pl.pallas_call(
        hold_kernel,
        out_shape=[shape(w.shape, BF) for w in weights],
        in_specs=anywhere(1 + len(weights)),
        out_specs=vmem(len(weights)),
        scratch_shapes=[pltpu.SemaphoreType.DMA((len(weights),))],
        compiler_params=params(40),
        name="hold_weights",
    )

    def worked_on(n):
        return [pltpu.VMEM((n * each, width), BF), pltpu.VMEM((n * each, width), F32)]

    near = pl.pallas_call(
        near_kernel,
        out_shape=[shape((rows, piece), BF)] * 2,
        in_specs=vmem(10),
        out_specs=vmem(2),
        scratch_shapes=worked_on(2),
        compiler_params=params(28),
        name="near_experts",
    )
    own = pl.pallas_call(
        own_kernel,
        out_shape=shape((rows, piece), BF),
        in_specs=vmem(5),
        out_specs=vmem(1)[0],
        scratch_shapes=worked_on(1),
        compiler_params=params(20),
        name="own_experts",
    )
    arrived = [swap(x) for x in outgoing]
    returned = []
    for x in arrived:
        held = hold(x, *weights)
        left, right = near(shift(x, 1), shift(x, -1), *held)
        mine = own(x, *held[:4])
        total = mine.astype(F32) + shift(left, -1).astype(F32) + shift(right, 1).astype(F32)
        returned.append(swap(total.astype(BF)))

    layer_out, mix = pl.pallas_call(
        combine_kernel,
        out_shape=[shape((block, width), BF)] * 2,
        in_specs=vmem(3 + chunks),
        out_specs=vmem(2),
        scratch_shapes=[pltpu.VMEM((each, width), BF)],
        compiler_params=params(16),
        name="combine",
    )(hidden, ids, gates, *returned)
    return layer_out[None], mix[None]


def solution(mesh):
    return jax.shard_map(
        per_device,
        mesh=mesh,
        in_specs=(
            P("expert", None, "dp"),
            P("expert", None, "dp"),
            P("expert", None, None),
            P("expert", None, None),
            P("expert", "dp", None, None),
            P("expert", "dp", None),
            P("expert", None),
            P("expert"),
            P("expert", None, None),
            P("dp", None, None),
            P("dp", None, None),
            P("dp", None),
            P(),
            P("expert", "dp", None, None),
            P("expert", "dp", None),
            P("expert", None, None),
            P("expert", None, None),
        ),
        out_specs=(P("expert", "dp", None), P("expert", "dp", None)),
        check_vma=False,
    )
```

```python
import functools

import jax
import jax.numpy as jnp
from jax import lax
from jax.experimental import pallas as pl
from jax.experimental.pallas import tpu as pltpu
from jax.sharding import PartitionSpec as P

HD = 128
RD = 64
LAT = 512
TOP = 6
PAGE = 64
EPS = 1e-06
NEG = -1e30

PIECES = 8
SLOTS = 3
SOME = 32
BLOCK = SOME * PIECES
BF = jnp.bfloat16
F32 = jnp.float32


def mm(a, b):
    return jnp.dot(a, b, preferred_element_type=F32)


def mm_nt(a, b):
    return lax.dot_general(a, b, (((1,), (1,)), ((), ())), preferred_element_type=F32)


def mm_tn(a, b):
    return lax.dot_general(a, b, (((0,), (0,)), ((), ())), preferred_element_type=F32)


def vmem(n):
    return [pl.BlockSpec(memory_space=pltpu.VMEM) for _ in range(n)]


def anywhere(n):
    return [pl.BlockSpec(memory_space=pl.ANY) for _ in range(n)]


def start_all(sources, targets, sems):
    copies = [
        pltpu.make_async_copy(a, b, sems.at[i]) for i, (a, b) in enumerate(zip(sources, targets))
    ]
    for copy in copies:
        copy.start()
    return copies


def params(mib):
    return pltpu.CompilerParams(vmem_limit_bytes=mib * 2**20)


def split_kernel(pairs, out):
    out[0] = pairs[0, :, 0, :]
    out[1] = pairs[0, :, 1, :]


def attend_kernel(facts, *refs):
    given, out, (q_scr, ho_scr), held, sems = refs[:11], refs[11], refs[12:14], refs[14:25], refs[25]
    copies = start_all(given, held, sems)
    qn, ku, qr, ln, kr, k0, k1, k2, k3, vu, ow = held
    tokens = qn.shape[0]
    heads = ku.shape[0]
    width = q_scr.shape[1]
    span = k0.shape[0]
    pages = facts.shape[0] - 2
    here = span // PAGE
    for copy in copies[:3]:
        copy.wait()
    for h in range(heads):
        rows = pl.ds(h * tokens, tokens)
        q_scr[rows, 0:LAT] = mm(qn[:, h * HD : (h + 1) * HD], ku[h]).astype(BF)
        rope = qr[:, h * RD : (h + 1) * RD]
        q_scr[rows, LAT:width] = jnp.concatenate(
            [rope, jnp.zeros((tokens, width - LAT - RD), BF)], axis=1
        )
    keys = (k0, k1, k2, k3)
    lane = lax.broadcasted_iota(jnp.int32, (1, span), 1)
    bias = []
    for hop in (0, len(keys) - 1, 1, 2):
        holder = lax.rem(facts[pages + 1] + hop, len(keys))
        first = jnp.zeros((1, span), jnp.int32)
        for i in range(here):
            place = 0
            for j in range(pages):
                place = place + jnp.where(facts[j] == holder * here + i, j, 0)
            first = jnp.where(lane // PAGE == i, place * PAGE, first)
        bias.append(jnp.where(first + lax.rem(lane, PAGE) < facts[pages], 0.0, NEG))
    scale = 1.0 / (HD + RD) ** 0.5
    step = 2
    for h0 in range(0, heads, step):
        n = step * tokens
        q = q_scr[pl.ds(h0 * tokens, n), :]
        row = lax.rem(lax.broadcasted_iota(jnp.int32, (n, tokens), 0), tokens)
        col = lax.broadcasted_iota(jnp.int32, (n, tokens), 1)
        if h0 == 0:
            for copy in copies[3:9]:
                copy.wait()
        s_new = mm_nt(q[:, 0:LAT], ln[...]) + mm(q[:, LAT : LAT + RD], kr[...])
        s_new = jnp.where(col <= row, s_new * scale, NEG)
        s_old = [mm_nt(q, k[...]) * scale + b for k, b in zip(keys, bias)]
        peak = jnp.max(s_new, axis=1, keepdims=True)
        for s in s_old:
            peak = jnp.maximum(peak, jnp.max(s, axis=1, keepdims=True))
        e = jnp.exp(s_new - peak)
        total = jnp.sum(e, axis=1, keepdims=True)
        acc = mm(e.astype(BF), ln[...])
        for s, k in zip(s_old, keys):
            e = jnp.exp(s - peak)
            total = total + jnp.sum(e, axis=1, keepdims=True)
            acc = acc + mm(e.astype(BF), k[:, 0:LAT])
        latent = (acc / total).astype(BF)
        if h0 == 0:
            copies[9].wait()
        for i in range(step):
            ho_scr[:, (h0 + i) * HD : (h0 + i + 1) * HD] = mm(
                latent[i * tokens : (i + 1) * tokens], vu[h0 + i]
            ).astype(BF)
    copies[10].wait()
    for c in range(0, out.shape[1], 512):
        out[:, c : c + 512] = mm(ho_scr[...], ow[:, c : c + 512]).astype(BF)


def count_named(ids, experts):
    block = ids.shape[1]
    expert = lax.broadcasted_iota(jnp.int32, (experts, block), 0)
    named = jnp.zeros((experts, block), F32)
    for k in range(TOP):
        named = named + (ids[k : k + 1, :] == expert).astype(F32)
    a = lax.broadcasted_iota(jnp.int32, (block, block), 0)
    b = lax.broadcasted_iota(jnp.int32, (block, block), 1)
    rank = mm(named.astype(BF), (a < b).astype(BF))
    return jnp.where(named > 0, rank, -1.0)


def by_row(values, total):
    experts = values.shape[0]
    r = lax.broadcasted_iota(jnp.int32, (total, experts), 0)
    c = lax.broadcasted_iota(jnp.int32, (total, experts), 1)
    return mm((r // SLOTS == c).astype(BF), values.astype(BF))


def in_slot(rank_rows, chunk):
    slot = lax.rem(lax.broadcasted_iota(jnp.int32, rank_rows.shape, 0), SLOTS) + chunk * SLOTS
    return rank_rows == slot.astype(F32)


def reorder(transposed):
    i = lax.broadcasted_iota(jnp.int32, (BLOCK, BLOCK), 1 if transposed else 0)
    j = lax.broadcasted_iota(jnp.int32, (BLOCK, BLOCK), 0 if transposed else 1)
    return (j == lax.rem(i, SOME) * PIECES + i // SOME).astype(BF)


def unpack_rows(there, x, rows, base):
    w = x.shape[1]
    for b in range(x.shape[0] // BLOCK):
        out = mm(there, x[b * BLOCK : (b + 1) * BLOCK, :]).astype(BF)
        for p in range(PIECES):
            rows[pl.ds(base + b * SOME, SOME), p * w : (p + 1) * w] = out[
                p * SOME : (p + 1) * SOME
            ]


def pack_rows(back, rows, base, y):
    w = y.shape[1]
    for b in range(y.shape[0] // BLOCK):
        stacked = jnp.concatenate(
            [
                rows[pl.ds(base + b * SOME, SOME), p * w : (p + 1) * w].astype(BF)
                for p in range(PIECES)
            ],
            axis=0,
        )
        y[b * BLOCK : (b + 1) * BLOCK, :] = mm(back, stacked).astype(BF)


def pack_chunk(normed, ids, chunk, rows, stage):
    experts = rows.shape[0] // SLOTS
    rank_rows = by_row(count_named(ids, experts), experts * SLOTS)
    rows[...] = mm(in_slot(rank_rows, chunk).astype(BF), normed).astype(BF)
    pack_rows(reorder(True), rows, 0, stage)


def pack_kernel(
    partial, residual, gain, ids, unused_a, unused_b, hidden_out, normed_out, out,
    hidden, normed, rows, stage, sems,
):
    attended = partial[0].astype(F32)
    for i in range(1, partial.shape[0]):
        attended = attended + partial[i].astype(F32)
    total = residual[...].astype(F32) + attended
    hidden[0] = total
    hidden[1] = jnp.zeros_like(total)
    power = jnp.mean(total * total, axis=1, keepdims=True)
    normed[...] = (total * lax.rsqrt(power + EPS) * gain[...]).astype(BF)
    copies = start_all((hidden, normed), (hidden_out, normed_out), sems)
    pack_chunk(normed[...], ids, 0, rows, stage)
    copies.append(pltpu.make_async_copy(stage, out, sems.at[2]))
    copies[-1].start()
    for copy in copies:
        copy.wait()


def pack_more_kernel(chunk, normed, ids, out, rows, stage, sem):
    pack_chunk(normed[...], ids, chunk, rows, stage)
    copy = pltpu.make_async_copy(stage, out, sem)
    copy.start()
    copy.wait()


def hidden_units(x, w):
    n = w.shape[0] // 2
    gate = mm_nt(x, w[0:n, :])
    up = mm_nt(x, w[n : 2 * n, :])
    return (gate / (1.0 + jnp.exp(-gate)) * up).astype(BF)


def hold_kernel(unused, *refs):
    n = len(refs) // 2
    for copy in start_all(refs[:n], refs[n : 2 * n], refs[-1]):
        copy.wait()


def near_kernel(xl, xr, ia, da, ib, db, fia, fda, fib, fdb, yl, yr, rows, acc):
    each = rows.shape[0] // 2
    there, back = reorder(False), reorder(True)
    for i, x in enumerate((xl, xr)):
        unpack_rows(there, x, rows, i * each)
    acc[...] = mm(hidden_units(rows[...], ia), da[...])
    acc[...] += mm(hidden_units(rows[...], ib), db[...])
    for i, (fi, fd, y) in enumerate(((fia, fda, yl), (fib, fdb, yr))):
        part = pl.ds(i * each, each)
        acc[part, :] += mm(hidden_units(rows[part, :], fi), fd[...])
        pack_rows(back, acc, i * each, y)


def own_kernel(x, ia, da, ib, db, y, rows, acc):
    there, back = reorder(False), reorder(True)
    unpack_rows(there, x, rows, 0)
    acc[...] = mm(hidden_units(rows[...], ia), da[...])
    acc[...] += mm(hidden_units(rows[...], ib), db[...])
    pack_rows(back, acc, 0, y)


def combine_kernel(chunk, base, ids, gates, returned, *rest):
    outs, rows = rest[:-1], rest[-1]
    experts = rows.shape[0] // SLOTS
    rank = count_named(ids, experts)
    expert = lax.broadcasted_iota(jnp.int32, rank.shape, 0)
    gate = jnp.zeros(rank.shape, F32)
    for k in range(TOP):
        gate = gate + jnp.where(ids[k : k + 1, :] == expert, gates[k : k + 1, :], 0.0)
    high = gate.astype(BF).astype(F32)
    total = experts * SLOTS
    rank_rows, high_rows, low_rows = by_row(rank, total), by_row(high, total), by_row(gate - high, total)
    unpack_rows(reorder(False), returned, rows, 0)
    here = in_slot(rank_rows, chunk)
    mixed = None
    for factor in (high_rows, low_rows):
        term = mm_tn(jnp.where(here, factor, 0.0).astype(BF), rows[...])
        mixed = term if mixed is None else mixed + term
    if len(outs) == 1:
        outs[0][0] = base[0]
        outs[0][1] = base[1] + mixed
    else:
        mixed = base[1] + mixed
        outs[0][...] = (base[0] + mixed).astype(BF)
        outs[1][...] = mixed.astype(BF)


def per_device(
    query_nope,
    query_rope,
    latent_new,
    key_rope,
    latent_pages,
    rope_pages,
    page_table,
    prefix_lengths,
    residual,
    key_up,
    value_up,
    out_weight,
    norm_gain,
    expert_in,
    expert_down,
    expert_ids,
    expert_weights,
):
    groups = lax.axis_size("dp")
    experts = lax.axis_size("expert")
    me = lax.axis_index("dp")
    tokens, width = residual.shape[1:]
    block = tokens // groups
    span = latent_pages.shape[1] * PAGE
    chunks = TOP // SLOTS
    rows = experts * SLOTS * PIECES
    piece = width // PIECES
    shape = jax.ShapeDtypeStruct

    def shift(x, k):
        return lax.ppermute(x, "dp", [(i, (i + k) % groups) for i in range(groups)])

    pad = LAT // 4 - RD
    keys = jnp.concatenate(
        [
            latent_pages[0].reshape(span, LAT),
            rope_pages[0].reshape(span, RD),
            jnp.zeros((span, pad), BF),
        ],
        axis=1,
    )
    from_left, from_right, from_far = shift(keys, 1), shift(keys, -1), shift(keys, 2)

    facts = jnp.concatenate([page_table[0], prefix_lengths, me.astype(jnp.int32)[None]])

    start = me * block
    ids = lax.dynamic_slice_in_dim(expert_ids[0], start, block, 0)
    gates = lax.dynamic_slice_in_dim(expert_weights[0], start, block, 0)
    residual_mine = lax.dynamic_slice_in_dim(residual[0], start, block, 0)
    ids, gates = ids.T, gates.T

    half = expert_in.shape[1] // 2

    def split_half(x, i):
        rows_in = pl.pallas_call(
            split_kernel,
            grid=(1,),
            out_shape=shape((2, half, width), BF),
            in_specs=[pl.BlockSpec((1, half, 2, width), lambda j: (0, i, 0, 0))],
            out_specs=pl.BlockSpec((2, half, width), lambda j: (0, 0, 0)),
            compiler_params=params(56),
            name="split_rows",
        )(x)
        return rows_in.reshape(2 * half, width)

    ia = split_half(expert_in, 0)
    da, db = expert_down[0, :half, :], expert_down[0, half:, :]
    send_da, send_db, ia, from_far = lax.optimization_barrier((da, db, ia, from_far))
    far_da, far_db = shift(send_da, -1), shift(send_db, 1)

    given = (
        query_nope[0],
        key_up,
        query_rope[0],
        latent_new[0],
        key_rope[0].T,
        keys,
        from_left,
        from_right,
        from_far,
        value_up,
        out_weight,
    )
    partial = pl.pallas_call(
        attend_kernel,
        out_shape=shape((tokens, width), BF),
        in_specs=[pl.BlockSpec(memory_space=pltpu.SMEM)] + anywhere(len(given)),
        out_specs=vmem(1)[0],
        scratch_shapes=[
            pltpu.VMEM((key_up.shape[0] * tokens, keys.shape[1]), BF),
            pltpu.VMEM((tokens, key_up.shape[0] * HD), BF),
        ]
        + [pltpu.VMEM(x.shape, BF) for x in given]
        + [pltpu.SemaphoreType.DMA((len(given),))],
        compiler_params=params(56),
        name="attend",
    )(facts, *given)
    later_in, partial = lax.optimization_barrier((expert_in, partial))
    ib = split_half(later_in, 1)
    partial = lax.all_to_all(
        partial.reshape(groups, block, width), "dp", split_axis=0, concat_axis=0, tiled=True
    )
    send_ia, send_ib, partial = lax.optimization_barrier((ia, ib, partial))
    far_ia, far_ib = shift(send_ia, -1), shift(send_ib, 1)
    packing = [pltpu.VMEM((SLOTS * experts, width), BF), pltpu.VMEM((rows, piece), BF)]
    hidden, normed, first = pl.pallas_call(
        pack_kernel,
        out_shape=[
            shape((2, block, width), F32),
            shape((block, width), BF),
            shape((rows, piece), BF),
        ],
        in_specs=vmem(4) + anywhere(2),
        out_specs=anywhere(3),
        scratch_shapes=[pltpu.VMEM((2, block, width), F32), pltpu.VMEM((block, width), BF)]
        + packing
        + [pltpu.SemaphoreType.DMA((3,))],
        compiler_params=params(56),
        name="pack",
    )(partial, residual_mine, norm_gain.reshape(1, width), ids, far_da, far_db)
    outgoing = [first] + [
        pl.pallas_call(
            functools.partial(pack_more_kernel, i),
            out_shape=shape((rows, piece), BF),
            in_specs=vmem(2),
            out_specs=anywhere(1)[0],
            scratch_shapes=packing + [pltpu.SemaphoreType.DMA],
            compiler_params=params(56),
            name="pack_more",
        )(normed, ids)
        for i in range(1, chunks)
    ]

    def swap(x):
        x = x.reshape(experts, SLOTS * PIECES, piece)
        x = lax.all_to_all(x, "expert", split_axis=0, concat_axis=0, tiled=True)
        return x.reshape(rows, piece)

    each = SLOTS * experts

    weights = (ia, da, ib, db, far_ia, far_da, far_ib, far_db)
    hold = pl.pallas_call(
        hold_kernel,
        out_shape=[shape(w.shape, BF) for w in weights],
        in_specs=anywhere(1 + len(weights)),
        out_specs=vmem(len(weights)),
        scratch_shapes=[pltpu.SemaphoreType.DMA((len(weights),))],
        compiler_params=params(40),
        name="hold_weights",
    )

    def worked_on(n):
        return [pltpu.VMEM((n * each, width), BF), pltpu.VMEM((n * each, width), F32)]

    near = pl.pallas_call(
        near_kernel,
        out_shape=[shape((rows, piece), BF)] * 2,
        in_specs=vmem(10),
        out_specs=vmem(2),
        scratch_shapes=worked_on(2),
        compiler_params=params(28),
        name="near_experts",
    )
    own = pl.pallas_call(
        own_kernel,
        out_shape=shape((rows, piece), BF),
        in_specs=vmem(5),
        out_specs=vmem(1)[0],
        scratch_shapes=worked_on(1),
        compiler_params=params(20),
        name="own_experts",
    )
    arrived = [swap(x) for x in outgoing]
    returned = []
    state = [hidden]
    for x in arrived:
        held = hold(x, *weights)
        left, right = near(shift(x, 1), shift(x, -1), *held)
        mine = own(x, *held[:4])
        total = mine.astype(F32) + shift(left, -1).astype(F32) + shift(right, 1).astype(F32)
        returned.append(swap(total.astype(BF)))

    for i, x in enumerate(returned):
        last = i + 1 == chunks
        state = pl.pallas_call(
            functools.partial(combine_kernel, i),
            out_shape=[shape((block, width), BF)] * 2 if last else [shape((2, block, width), F32)],
            in_specs=vmem(4),
            out_specs=vmem(2 if last else 1),
            scratch_shapes=[pltpu.VMEM((each, width), BF)],
            compiler_params=params(16),
            name="combine",
        )(state[0], ids, gates, x)
    layer_out, mix = state
    return layer_out[None], mix[None]


def solution(mesh):
    return jax.shard_map(
        per_device,
        mesh=mesh,
        in_specs=(
            P("expert", None, "dp"),
            P("expert", None, "dp"),
            P("expert", None, None),
            P("expert", None, None),
            P("expert", "dp", None, None),
            P("expert", "dp", None),
            P("expert", None),
            P("expert"),
            P("expert", None, None),
            P("dp", None, None),
            P("dp", None, None),
            P("dp", None),
            P(),
            P("expert", "dp", None, None),
            P("expert", "dp", None),
            P("expert", None, None),
            P("expert", None, None),
        ),
        out_specs=(P("expert", "dp", None), P("expert", "dp", None)),
        check_vma=False,
    )
```

```python
import functools

import jax
import jax.numpy as jnp
from jax import lax
from jax.experimental import pallas as pl
from jax.experimental.pallas import tpu as pltpu
from jax.sharding import PartitionSpec as P

HD = 128
RD = 64
LAT = 512
TOP = 6
PAGE = 64
EPS = 1e-06
NEG = -1e30

PIECES = 8
SLOTS = 3
SOME = 32
BLOCK = SOME * PIECES
BF = jnp.bfloat16
F32 = jnp.float32


def mm(a, b):
    return jnp.dot(a, b, preferred_element_type=F32)


def mm_nt(a, b):
    return lax.dot_general(a, b, (((1,), (1,)), ((), ())), preferred_element_type=F32)


def mm_tn(a, b):
    return lax.dot_general(a, b, (((0,), (0,)), ((), ())), preferred_element_type=F32)


def vmem(n):
    return [pl.BlockSpec(memory_space=pltpu.VMEM) for _ in range(n)]


def anywhere(n):
    return [pl.BlockSpec(memory_space=pl.ANY) for _ in range(n)]


def start_all(sources, targets, sems):
    copies = [
        pltpu.make_async_copy(a, b, sems.at[i]) for i, (a, b) in enumerate(zip(sources, targets))
    ]
    for copy in copies:
        copy.start()
    return copies


def params(mib):
    return pltpu.CompilerParams(vmem_limit_bytes=mib * 2**20)


def split_kernel(pairs, out):
    out[0] = pairs[0, :, 0, :]
    out[1] = pairs[0, :, 1, :]


def attend_kernel(facts, *refs):
    given, out, (q_scr, ho_scr), held, sems = refs[:11], refs[11], refs[12:14], refs[14:25], refs[25]
    copies = start_all(given, held, sems)
    qn, ku, qr, ln, kr, k0, k1, k2, k3, vu, ow = held
    tokens = qn.shape[0]
    heads = ku.shape[0]
    width = q_scr.shape[1]
    span = k0.shape[0]
    pages = facts.shape[0] - 2
    here = span // PAGE
    for copy in copies[:3]:
        copy.wait()
    for h in range(heads):
        rows = pl.ds(h * tokens, tokens)
        q_scr[rows, 0:LAT] = mm(qn[:, h * HD : (h + 1) * HD], ku[h]).astype(BF)
        rope = qr[:, h * RD : (h + 1) * RD]
        q_scr[rows, LAT:width] = jnp.concatenate(
            [rope, jnp.zeros((tokens, width - LAT - RD), BF)], axis=1
        )
    keys = (k0, k1, k2, k3)
    lane = lax.broadcasted_iota(jnp.int32, (1, span), 1)
    bias = []
    for hop in (0, len(keys) - 1, 1, 2):
        holder = lax.rem(facts[pages + 1] + hop, len(keys))
        first = jnp.zeros((1, span), jnp.int32)
        for i in range(here):
            place = 0
            for j in range(pages):
                place = place + jnp.where(facts[j] == holder * here + i, j, 0)
            first = jnp.where(lane // PAGE == i, place * PAGE, first)
        bias.append(jnp.where(first + lax.rem(lane, PAGE) < facts[pages], 0.0, NEG))
    scale = 1.0 / (HD + RD) ** 0.5
    step = 2
    for h0 in range(0, heads, step):
        n = step * tokens
        q = q_scr[pl.ds(h0 * tokens, n), :]
        row = lax.rem(lax.broadcasted_iota(jnp.int32, (n, tokens), 0), tokens)
        col = lax.broadcasted_iota(jnp.int32, (n, tokens), 1)
        if h0 == 0:
            for copy in copies[3:9]:
                copy.wait()
        s_new = mm_nt(q[:, 0:LAT], ln[...]) + mm(q[:, LAT : LAT + RD], kr[...])
        s_new = jnp.where(col <= row, s_new * scale, NEG)
        s_old = [mm_nt(q, k[...]) * scale + b for k, b in zip(keys, bias)]
        peak = jnp.max(s_new, axis=1, keepdims=True)
        for s in s_old:
            peak = jnp.maximum(peak, jnp.max(s, axis=1, keepdims=True))
        e = jnp.exp(s_new - peak)
        total = jnp.sum(e, axis=1, keepdims=True)
        acc = mm(e.astype(BF), ln[...])
        for s, k in zip(s_old, keys):
            e = jnp.exp(s - peak)
            total = total + jnp.sum(e, axis=1, keepdims=True)
            acc = acc + mm(e.astype(BF), k[:, 0:LAT])
        latent = (acc / total).astype(BF)
        if h0 == 0:
            copies[9].wait()
        for i in range(step):
            ho_scr[:, (h0 + i) * HD : (h0 + i + 1) * HD] = mm(
                latent[i * tokens : (i + 1) * tokens], vu[h0 + i]
            ).astype(BF)
    copies[10].wait()
    for c in range(0, out.shape[1], 512):
        out[:, c : c + 512] = mm(ho_scr[...], ow[:, c : c + 512]).astype(BF)


def count_named(ids, experts):
    block = ids.shape[1]
    expert = lax.broadcasted_iota(jnp.int32, (experts, block), 0)
    named = jnp.zeros((experts, block), F32)
    for k in range(TOP):
        named = named + (ids[k : k + 1, :] == expert).astype(F32)
    a = lax.broadcasted_iota(jnp.int32, (block, block), 0)
    b = lax.broadcasted_iota(jnp.int32, (block, block), 1)
    rank = mm(named.astype(BF), (a < b).astype(BF))
    return jnp.where(named > 0, rank, -1.0)


def by_row(values, total):
    experts = values.shape[0]
    r = lax.broadcasted_iota(jnp.int32, (total, experts), 0)
    c = lax.broadcasted_iota(jnp.int32, (total, experts), 1)
    return mm((r // SLOTS == c).astype(BF), values.astype(BF))


def in_slot(rank_rows, chunk):
    slot = lax.rem(lax.broadcasted_iota(jnp.int32, rank_rows.shape, 0), SLOTS) + chunk * SLOTS
    return rank_rows == slot.astype(F32)


def reorder(transposed):
    i = lax.broadcasted_iota(jnp.int32, (BLOCK, BLOCK), 1 if transposed else 0)
    j = lax.broadcasted_iota(jnp.int32, (BLOCK, BLOCK), 0 if transposed else 1)
    return (j == lax.rem(i, SOME) * PIECES + i // SOME).astype(BF)


def unpack_rows(there, x, rows, base):
    w = x.shape[1]
    for b in range(x.shape[0] // BLOCK):
        out = mm(there, x[b * BLOCK : (b + 1) * BLOCK, :]).astype(BF)
        for p in range(PIECES):
            rows[pl.ds(base + b * SOME, SOME), p * w : (p + 1) * w] = out[
                p * SOME : (p + 1) * SOME
            ]


def pack_rows(back, rows, base, y):
    w = y.shape[1]
    for b in range(y.shape[0] // BLOCK):
        stacked = jnp.concatenate(
            [
                rows[pl.ds(base + b * SOME, SOME), p * w : (p + 1) * w].astype(BF)
                for p in range(PIECES)
            ],
            axis=0,
        )
        y[b * BLOCK : (b + 1) * BLOCK, :] = mm(back, stacked).astype(BF)


def pack_chunk(normed, ids, chunk, rows, stage):
    experts = rows.shape[0] // SLOTS
    rank_rows = by_row(count_named(ids, experts), experts * SLOTS)
    rows[...] = mm(in_slot(rank_rows, chunk).astype(BF), normed).astype(BF)
    pack_rows(reorder(True), rows, 0, stage)


def pack_kernel(
    partial, residual, gain, ids, hidden_out, normed_out, out,
    hidden, normed, rows, stage, sems,
):
    attended = partial[0].astype(F32)
    for i in range(1, partial.shape[0]):
        attended = attended + partial[i].astype(F32)
    total = residual[...].astype(F32) + attended
    hidden[0] = total
    hidden[1] = jnp.zeros_like(total)
    power = jnp.mean(total * total, axis=1, keepdims=True)
    normed[...] = (total * lax.rsqrt(power + EPS) * gain[...]).astype(BF)
    copies = start_all((hidden, normed), (hidden_out, normed_out), sems)
    pack_chunk(normed[...], ids, 0, rows, stage)
    copies.append(pltpu.make_async_copy(stage, out, sems.at[2]))
    copies[-1].start()
    for copy in copies:
        copy.wait()


def pack_more_kernel(chunk, normed, ids, unused_a, unused_b, out, rows, stage, sem):
    pack_chunk(normed[...], ids, chunk, rows, stage)
    copy = pltpu.make_async_copy(stage, out, sem)
    copy.start()
    copy.wait()


def hidden_units(x, w):
    n = w.shape[0] // 2
    gate = mm_nt(x, w[0:n, :])
    up = mm_nt(x, w[n : 2 * n, :])
    return (gate / (1.0 + jnp.exp(-gate)) * up).astype(BF)


def hold_kernel(unused, *refs):
    n = len(refs) // 2
    for copy in start_all(refs[:n], refs[n : 2 * n], refs[-1]):
        copy.wait()


def near_kernel(xl, xr, ia, da, ib, db, fia, fda, fib, fdb, yl, yr, rows, acc):
    each = rows.shape[0] // 2
    there, back = reorder(False), reorder(True)
    for i, x in enumerate((xl, xr)):
        unpack_rows(there, x, rows, i * each)
    acc[...] = mm(hidden_units(rows[...], ia), da[...])
    acc[...] += mm(hidden_units(rows[...], ib), db[...])
    for i, (fi, fd, y) in enumerate(((fia, fda, yl), (fib, fdb, yr))):
        part = pl.ds(i * each, each)
        acc[part, :] += mm(hidden_units(rows[part, :], fi), fd[...])
        pack_rows(back, acc, i * each, y)


def own_kernel(x, ia, da, ib, db, y, rows, acc):
    there, back = reorder(False), reorder(True)
    unpack_rows(there, x, rows, 0)
    acc[...] = mm(hidden_units(rows[...], ia), da[...])
    acc[...] += mm(hidden_units(rows[...], ib), db[...])
    pack_rows(back, acc, 0, y)


def combine_kernel(chunk, base, ids, gates, returned, *rest):
    outs, rows = rest[:-1], rest[-1]
    experts = rows.shape[0] // SLOTS
    rank = count_named(ids, experts)
    expert = lax.broadcasted_iota(jnp.int32, rank.shape, 0)
    gate = jnp.zeros(rank.shape, F32)
    for k in range(TOP):
        gate = gate + jnp.where(ids[k : k + 1, :] == expert, gates[k : k + 1, :], 0.0)
    high = gate.astype(BF).astype(F32)
    total = experts * SLOTS
    rank_rows, high_rows, low_rows = by_row(rank, total), by_row(high, total), by_row(gate - high, total)
    unpack_rows(reorder(False), returned, rows, 0)
    here = in_slot(rank_rows, chunk)
    mixed = None
    for factor in (high_rows, low_rows):
        term = mm_tn(jnp.where(here, factor, 0.0).astype(BF), rows[...])
        mixed = term if mixed is None else mixed + term
    if len(outs) == 1:
        outs[0][0] = base[0]
        outs[0][1] = base[1] + mixed
    else:
        mixed = base[1] + mixed
        outs[0][...] = (base[0] + mixed).astype(BF)
        outs[1][...] = mixed.astype(BF)


def per_device(
    query_nope,
    query_rope,
    latent_new,
    key_rope,
    latent_pages,
    rope_pages,
    page_table,
    prefix_lengths,
    residual,
    key_up,
    value_up,
    out_weight,
    norm_gain,
    expert_in,
    expert_down,
    expert_ids,
    expert_weights,
):
    groups = lax.axis_size("dp")
    experts = lax.axis_size("expert")
    me = lax.axis_index("dp")
    tokens, width = residual.shape[1:]
    block = tokens // groups
    span = latent_pages.shape[1] * PAGE
    chunks = TOP // SLOTS
    rows = experts * SLOTS * PIECES
    piece = width // PIECES
    shape = jax.ShapeDtypeStruct

    def shift(x, k):
        return lax.ppermute(x, "dp", [(i, (i + k) % groups) for i in range(groups)])

    pad = LAT // 4 - RD
    keys = jnp.concatenate(
        [
            latent_pages[0].reshape(span, LAT),
            rope_pages[0].reshape(span, RD),
            jnp.zeros((span, pad), BF),
        ],
        axis=1,
    )
    from_left, from_right, from_far = shift(keys, 1), shift(keys, -1), shift(keys, 2)

    facts = jnp.concatenate([page_table[0], prefix_lengths, me.astype(jnp.int32)[None]])

    start = me * block
    ids = lax.dynamic_slice_in_dim(expert_ids[0], start, block, 0)
    gates = lax.dynamic_slice_in_dim(expert_weights[0], start, block, 0)
    residual_mine = lax.dynamic_slice_in_dim(residual[0], start, block, 0)
    ids, gates = ids.T, gates.T

    half = expert_in.shape[1] // 2

    def split_half(x, i):
        rows_in = pl.pallas_call(
            split_kernel,
            grid=(1,),
            out_shape=shape((2, half, width), BF),
            in_specs=[pl.BlockSpec((1, half, 2, width), lambda j: (0, i, 0, 0))],
            out_specs=pl.BlockSpec((2, half, width), lambda j: (0, 0, 0)),
            compiler_params=params(56),
            name="split_rows",
        )(x)
        return rows_in.reshape(2 * half, width)

    ia = split_half(expert_in, 0)
    da, db = expert_down[0, :half, :], expert_down[0, half:, :]
    send_da, send_db, ia, from_far = lax.optimization_barrier((da, db, ia, from_far))
    far_da, far_db = shift(send_da, -1), shift(send_db, 1)

    given = (
        query_nope[0],
        key_up,
        query_rope[0],
        latent_new[0],
        key_rope[0].T,
        keys,
        from_left,
        from_right,
        from_far,
        value_up,
        out_weight,
    )
    partial = pl.pallas_call(
        attend_kernel,
        out_shape=shape((tokens, width), BF),
        in_specs=[pl.BlockSpec(memory_space=pltpu.SMEM)] + anywhere(len(given)),
        out_specs=vmem(1)[0],
        scratch_shapes=[
            pltpu.VMEM((key_up.shape[0] * tokens, keys.shape[1]), BF),
            pltpu.VMEM((tokens, key_up.shape[0] * HD), BF),
        ]
        + [pltpu.VMEM(x.shape, BF) for x in given]
        + [pltpu.SemaphoreType.DMA((len(given),))],
        compiler_params=params(56),
        name="attend",
    )(facts, *given)
    later_in, partial = lax.optimization_barrier((expert_in, partial))
    ib = split_half(later_in, 1)
    partial = lax.all_to_all(
        partial.reshape(groups, block, width), "dp", split_axis=0, concat_axis=0, tiled=True
    )
    send_ia, send_ib, partial = lax.optimization_barrier((ia, ib, partial))
    far_ia, far_ib = shift(send_ia, -1), shift(send_ib, 1)
    packing = [pltpu.VMEM((SLOTS * experts, width), BF), pltpu.VMEM((rows, piece), BF)]
    hidden, normed, first = pl.pallas_call(
        pack_kernel,
        out_shape=[
            shape((2, block, width), F32),
            shape((block, width), BF),
            shape((rows, piece), BF),
        ],
        in_specs=vmem(4),
        out_specs=anywhere(3),
        scratch_shapes=[pltpu.VMEM((2, block, width), F32), pltpu.VMEM((block, width), BF)]
        + packing
        + [pltpu.SemaphoreType.DMA((3,))],
        compiler_params=params(56),
        name="pack",
    )(partial, residual_mine, norm_gain.reshape(1, width), ids)
    outgoing = [first] + [
        pl.pallas_call(
            functools.partial(pack_more_kernel, i),
            out_shape=shape((rows, piece), BF),
            in_specs=vmem(2) + anywhere(2),
            out_specs=anywhere(1)[0],
            scratch_shapes=packing + [pltpu.SemaphoreType.DMA],
            compiler_params=params(56),
            cost_estimate=pl.CostEstimate(flops=100_000_000_000, bytes_accessed=400 * 2**20, transcendentals=0),
            name="pack_more",
        )(normed, ids, far_da, far_db)
        for i in range(1, chunks)
    ]

    def swap(x):
        x = x.reshape(experts, SLOTS * PIECES, piece)
        x = lax.all_to_all(x, "expert", split_axis=0, concat_axis=0, tiled=True)
        return x.reshape(rows, piece)

    each = SLOTS * experts

    weights = (ia, da, ib, db, far_ia, far_da, far_ib, far_db)
    hold = pl.pallas_call(
        hold_kernel,
        out_shape=[shape(w.shape, BF) for w in weights],
        in_specs=anywhere(1 + len(weights)),
        out_specs=vmem(len(weights)),
        scratch_shapes=[pltpu.SemaphoreType.DMA((len(weights),))],
        compiler_params=params(40),
        name="hold_weights",
    )

    def worked_on(n):
        return [pltpu.VMEM((n * each, width), BF), pltpu.VMEM((n * each, width), F32)]

    near = pl.pallas_call(
        near_kernel,
        out_shape=[shape((rows, piece), BF)] * 2,
        in_specs=vmem(10),
        out_specs=vmem(2),
        scratch_shapes=worked_on(2),
        compiler_params=params(28),
        name="near_experts",
    )
    own = pl.pallas_call(
        own_kernel,
        out_shape=shape((rows, piece), BF),
        in_specs=vmem(5),
        out_specs=vmem(1)[0],
        scratch_shapes=worked_on(1),
        compiler_params=params(20),
        name="own_experts",
    )
    arrived = [swap(x) for x in outgoing]
    returned = []
    state = [hidden]
    for x in arrived:
        held = hold(x, *weights)
        left, right = near(shift(x, 1), shift(x, -1), *held)
        mine = own(x, *held[:4])
        total = mine.astype(F32) + shift(left, -1).astype(F32) + shift(right, 1).astype(F32)
        returned.append(swap(total.astype(BF)))

    for i, x in enumerate(returned):
        last = i + 1 == chunks
        state = pl.pallas_call(
            functools.partial(combine_kernel, i),
            out_shape=[shape((block, width), BF)] * 2 if last else [shape((2, block, width), F32)],
            in_specs=vmem(4),
            out_specs=vmem(2 if last else 1),
            scratch_shapes=[pltpu.VMEM((each, width), BF)],
            compiler_params=params(16),
            name="combine",
        )(state[0], ids, gates, x)
    layer_out, mix = state
    return layer_out[None], mix[None]


def solution(mesh):
    return jax.shard_map(
        per_device,
        mesh=mesh,
        in_specs=(
            P("expert", None, "dp"),
            P("expert", None, "dp"),
            P("expert", None, None),
            P("expert", None, None),
            P("expert", "dp", None, None),
            P("expert", "dp", None),
            P("expert", None),
            P("expert"),
            P("expert", None, None),
            P("dp", None, None),
            P("dp", None, None),
            P("dp", None),
            P(),
            P("expert", "dp", None, None),
            P("expert", "dp", None),
            P("expert", None, None),
            P("expert", None, None),
        ),
        out_specs=(P("expert", "dp", None), P("expert", "dp", None)),
        check_vma=False,
    )
```
